512 devices in a mesh: dp: 4 (over x), ctx: 16 (over z), tp: 8 (over y, core).
Axes of the slice: x: 4, y: 4, z: 16, core: 2. Of those that a mesh axis runs over, the one named last changes fastest.
Arguments:
- conv_input: bfloat16 [4, 4096, 10240], P('dp', 'ctx', 'tp'), may hold values from -6 to 6
- step_raw: float32 [4, 4096, 128], P('dp', 'ctx', 'tp'), may hold values from -3 to 3
- doc_starts: int32 [4, 4096], P('dp', 'ctx'), may hold values 0 or 1
- decay_power: int32 [128], P('tp'), may hold values from 0 to 3
- conv_weight: bfloat16 [4, 10240], P(None, 'tp'), may hold values from -3 to 3
- conv_bias: float32 [10240], P('tp'), may hold values from -3 to 3
- step_bias: float32 [128], P('tp'), may hold values from -7.3 to -2.25
- skip_gain: float32 [128], P('tp'), may hold values from 0.1 to 4
- grad_out: bfloat16 [4, 4096, 8192], P('dp', 'ctx', 'tp'), may hold values from -6 to 6
Outputs:
- grad_input: bfloat16 [4, 4096, 10240], P('dp', 'ctx', 'tp')
- grad_step_raw: float32 [4, 4096, 128], P('dp', 'ctx', 'tp')
- grad_conv_weight: float32 [4, 8, 1280], P(None, 'tp', ('dp', 'ctx'))
- grad_conv_bias: float32 [8, 1280], P('tp', ('dp', 'ctx'))
The draws below stay inside these ranges and needn't reach their ends.
All inputs are finite; a program needn't handle non-finite values. No bound on the sum of `doc_starts` on one device may be relied on, other than what follows from the above.
Results may differ from the reference program's by a relative error of at most 0.017.
Values may be sent and summed in bfloat16 or wider, within the bound.
No kernel may reach another device: no remote copies, remote signals or barrier semaphores. Data moves between devices by JAX's collectives and lax.ppermute only.
A program may use at most 128 MiB of HBM per device.

```python
import math
import jax
import jax.numpy as jnp
from jax import lax

BLOCK = 128
GROUP_HEADS = 16
HEAD_WIDTH = 64
STATE = 128
KERNEL = 4
GROUPS = 8
HEADS = 128
CHANNELS = 1280
ALL_CHANNELS = 10240
LENGTH = 4096
BATCH = 4


def draw_step_raw(key, part):
    key = jax.random.fold_in(key, 11)
    values = jnp.clip(jax.random.normal(key, (BATCH, LENGTH, HEADS), jnp.float32), -3.0, 3.0)
    return values


def draw_step_bias(key, part):
    key = jax.random.fold_in(key, 23)
    spread = jax.random.uniform(key, (HEADS,), jnp.float32, math.log(0.001), math.log(0.1))
    initial = jnp.exp(spread)
    values = jnp.log(jnp.expm1(initial))
    return values


def draw_skip_gain(key, part):
    key = jax.random.fold_in(key, 37)
    lowest = 0.3
    highest = 3.0
    spread = jax.random.uniform(key, (HEADS,), jnp.float32, math.log(lowest), math.log(highest))
    return jnp.exp(spread)


def with_ends(drawn, rng, low, high):
    shape = drawn.shape
    spot = [jax.random.randint(jax.random.fold_in(rng, axis), (), 0, shape[axis]) for axis in range(len(shape))]
    drawn = drawn.at[tuple(spot)].set(low)
    longest = shape.index(max(shape))
    spot[longest] = (spot[longest] + 1) % shape[longest]
    return drawn.at[tuple(spot)].set(high)


def block_levels(rng, dims, shards, least, top_value):
    factor_of = 1.0
    for axis_at, shards_of in shards:
        heights = jax.random.uniform(jax.random.fold_in(jax.random.fold_in(rng, 6), axis_at), (shards_of,), jnp.float32, least / len(shards), top_value / len(shards))
        factor_of = factor_of * jnp.repeat(jnp.exp(heights), dims[axis_at] // shards_of).reshape((-1,) + (1,) * (len(dims) - 1 - axis_at))
    return factor_of


def centred(stream_key, extent, scale, most, shards=(), dtype=jnp.bfloat16):
    drawn = scale * jax.random.normal(stream_key, extent, jnp.float32)
    if shards:
        drawn = drawn * block_levels(stream_key, extent, shards, -0.22, 0.18)
    return jnp.clip(drawn, -most, most).astype(dtype)


def setup_inputs(seed: int = 0) -> dict:
    splits = jax.random.split(jax.random.key(seed), 10)
    conv_input = centred(splits[0], (BATCH, LENGTH, ALL_CHANNELS), 1.0, 6.0, ((0, 4), (1, 16), (2, 8)))
    step_raw = draw_step_raw(jax.random.fold_in(splits[9], 71), 0)
    doc_starts = with_ends((jax.random.randint(splits[2], (BATCH, LENGTH), 0, 2048) < 1).astype(jnp.int32), jax.random.fold_in(splits[2], 1), 0, 1)
    decay_power = with_ends(jax.random.randint(splits[3], (HEADS,), 0, 4), jax.random.fold_in(splits[3], 1), 0, 3).astype(jnp.int32)
    conv_weight = centred(splits[4], (KERNEL, ALL_CHANNELS), KERNEL ** -0.5, 3.0, ((1, 8),))
    conv_bias = centred(splits[5], (ALL_CHANNELS,), 0.5, 3.0, ((0, 8),), jnp.float32)
    step_bias = draw_step_bias(jax.random.fold_in(splits[9], 71), 0)
    skip_gain = draw_skip_gain(jax.random.fold_in(splits[9], 71), 0)
    grad_out = centred(splits[8], (BATCH, LENGTH, HEADS * HEAD_WIDTH), 1.0, 6.0, ((0, 4), (1, 16), (2, 8)))
    return {"conv_input": conv_input, "step_raw": step_raw, "doc_starts": doc_starts, "decay_power": decay_power, "conv_weight": conv_weight, "conv_bias": conv_bias, "step_bias": step_bias, "skip_gain": skip_gain, "grad_out": grad_out}


def decay_rates(decay_power, length):
    return -0.5 * jnp.exp((decay_power.astype(jnp.float32) / 3.0 - 1.0) * math.log(length))

def conv_activate(padded, weight32, bias):
    count = padded.shape[0] - (KERNEL - 1)
    total = bias[None, :] + padded[0:count] * weight32[0][None, :]
    for offset in range(1, KERNEL):
        total = total + padded[offset:offset + count] * weight32[offset][None, :]
    return jax.nn.silu(total).astype(jnp.bfloat16)

def split_channels(activated, heads):
    count = activated.shape[0]
    inner = heads * HEAD_WIDTH
    values = activated[:, :inner].reshape(count, heads, HEAD_WIDTH)
    keys = activated[:, inner:inner + STATE]
    queries = activated[:, inner + STATE:inner + 2 * STATE]
    return (values, keys, queries)

def block_prefix(decay_log, starts_block):
    cumulative = jnp.cumsum(decay_log, axis=0)
    doc_index = jnp.cumsum(starts_block)
    alive = (doc_index == 0.0).astype(jnp.float32)
    return (cumulative, doc_index, alive)

def block_state(state, values, keys, step_size, cumulative, doc_index, alive):
    tail = jnp.exp(cumulative[-1][None, :] - cumulative) * (doc_index == doc_index[-1]).astype(jnp.float32)[:, None]
    weighted = (values.astype(jnp.float32) * (step_size * tail)[:, :, None]).astype(jnp.bfloat16)
    fresh = jnp.einsum('shp,sn->hpn', weighted.astype(jnp.float32), keys.astype(jnp.float32), precision=lax.Precision.HIGHEST)
    return fresh + (jnp.exp(cumulative[-1]) * alive[-1])[:, None, None] * state

def block_step(state, pieces, skip_gain):
    activated, step_size, decay_log, starts_block = pieces
    heads = step_size.shape[1]
    count = activated.shape[0]
    values, keys, queries = split_channels(activated, heads)
    cumulative, doc_index, alive = block_prefix(decay_log, starts_block)
    positions = jnp.arange(count)
    lower = ((positions[:, None] >= positions[None, :]) & (doc_index[:, None] == doc_index[None, :])).astype(jnp.float32)
    across = cumulative.T
    gaps = jnp.minimum(across[:, :, None] - across[:, None, :], 0.0)
    scores = jnp.dot(queries, keys.T, preferred_element_type=jnp.float32)
    mixing = (scores[None] * jnp.exp(gaps) * lower[None] * step_size.T[:, None, :]).astype(jnp.bfloat16)
    local = jnp.einsum('hts,shp->thp', mixing.astype(jnp.float32), values.astype(jnp.float32), precision=lax.Precision.HIGHEST)
    carried = jnp.einsum('tn,hpn->thp', queries.astype(jnp.float32), state, precision=lax.Precision.HIGHEST)
    out_decay = jnp.exp(cumulative) * alive[:, None]
    result = local + out_decay[:, :, None] * carried + skip_gain[None, :, None] * values.astype(jnp.float32)
    following = block_state(state, values, keys, step_size, cumulative, doc_index, alive)
    return (following, result.reshape(count, heads * HEAD_WIDTH))

def run_blocks(state, activated, step_size, decay_log, flags, skip_gain):
    count = activated.shape[0]
    blocks = count // BLOCK
    pieces = (activated.reshape(blocks, BLOCK, activated.shape[1]), step_size.reshape(blocks, BLOCK, step_size.shape[1]), decay_log.reshape(blocks, BLOCK, decay_log.shape[1]), flags.reshape(blocks, BLOCK))
    final, outputs = lax.scan(lambda carry, item: block_step(carry, item, skip_gain), state, pieces)
    return (outputs.reshape(count, outputs.shape[2]), final)

def reference(conv_input, step_raw, doc_starts, decay_power, conv_weight, conv_bias, step_bias, skip_gain, grad_out):
    rates = decay_rates(decay_power, LENGTH)
    inner = GROUP_HEADS * HEAD_WIDTH

    def one_group(index):
        batch = (index // GROUPS).astype(jnp.int32)
        group = (index % GROUPS).astype(jnp.int32)
        zero = jnp.zeros((), jnp.int32)
        inputs32 = lax.dynamic_slice(conv_input, (batch, zero, group * CHANNELS), (1, LENGTH, CHANNELS))[0].astype(jnp.float32)
        raw = lax.dynamic_slice(step_raw, (batch, zero, group * GROUP_HEADS), (1, LENGTH, GROUP_HEADS))[0]
        flags = lax.dynamic_slice(doc_starts, (batch, zero), (1, LENGTH))[0].astype(jnp.float32)
        cotangent = lax.dynamic_slice(grad_out, (batch, zero, group * inner), (1, LENGTH, inner))[0].astype(jnp.float32)
        weight32 = lax.dynamic_slice(conv_weight, (zero, group * CHANNELS), (KERNEL, CHANNELS)).astype(jnp.float32)
        bias = lax.dynamic_slice(conv_bias, (group * CHANNELS,), (CHANNELS,))
        bias_step = lax.dynamic_slice(step_bias, (group * GROUP_HEADS,), (GROUP_HEADS,))
        skip_group = lax.dynamic_slice(skip_gain, (group * GROUP_HEADS,), (GROUP_HEADS,))
        rate_group = lax.dynamic_slice(rates, (group * GROUP_HEADS,), (GROUP_HEADS,))

        def forward(inputs_in, raw_in, weight_in, bias_in):
            padded = jnp.concatenate([jnp.zeros((KERNEL - 1, CHANNELS), jnp.float32), inputs_in], 0)
            activated = conv_activate(padded, weight_in, bias_in)
            step_size = jax.nn.softplus(raw_in + bias_step[None, :])
            start_state = jnp.zeros((GROUP_HEADS, HEAD_WIDTH, STATE), jnp.float32)
            result, final = run_blocks(start_state, activated, step_size, step_size * rate_group[None, :], flags, skip_group)
            return result
        result, pull = jax.vjp(forward, inputs32, raw, weight32, bias)
        grad_in, grad_raw, grad_weight, grad_bias = pull(cotangent)
        return (grad_in.astype(jnp.bfloat16), grad_raw, grad_weight, grad_bias)
    grad_in, grad_raw, grad_weight, grad_bias = lax.map(one_group, jnp.arange(BATCH * GROUPS).astype(jnp.int32))
    scale = 1.0 / (BATCH * LENGTH)
    grad_input = grad_in.reshape(BATCH, GROUPS, LENGTH, CHANNELS).transpose(0, 2, 1, 3).reshape(BATCH, LENGTH, GROUPS * CHANNELS)
    grad_step_raw = grad_raw.reshape(BATCH, GROUPS, LENGTH, GROUP_HEADS).transpose(0, 2, 1, 3).reshape(BATCH, LENGTH, HEADS)
    grad_conv_weight = lax.optimization_barrier(jnp.sum(grad_weight.reshape(BATCH, GROUPS, KERNEL, CHANNELS), axis=0)).transpose(1, 0, 2) * scale
    grad_conv_bias = lax.optimization_barrier(jnp.sum(grad_bias.reshape(BATCH, GROUPS, CHANNELS), axis=0)) * scale
    return (grad_input, grad_step_raw, grad_conv_weight, grad_conv_bias)
```

```python
import math

import jax
import jax.numpy as jnp
from jax import lax
from jax.experimental import pallas as pl
from jax.experimental.pallas import tpu as pltpu
from jax.sharding import PartitionSpec as P

BLOCK = 128
HEAD_WIDTH = 64
STATE = 128
KERNEL = 4
ROWS = 8
EXTRA = 128
VMEM_BYTES = 50 * 1024 * 1024
F32 = jnp.float32
BF16 = jnp.bfloat16


def mm(left, right):
    return jnp.dot(left, right, preferred_element_type=F32)


def mm_nt(left, right):
    return lax.dot_general(left, right, (((1,), (1,)), ((), ())), preferred_element_type=F32)


def mm_tn(left, right):
    return lax.dot_general(left, right, (((0,), (0,)), ((), ())), preferred_element_type=F32)


def pieces_of(value, count):
    out = []
    for _ in range(count):
        piece = value.astype(BF16)
        out.append(piece)
        value = value - piece.astype(F32)
    return out


def exact_left(ones, value, count):
    return sum(mm(ones, piece) for piece in pieces_of(value, count))


def exact_right(value, ones, count):
    return sum(mm(piece, ones) for piece in pieces_of(value, count))


def spread_matrix(rows, columns):
    row = lax.broadcasted_iota(jnp.int32, (rows, columns), 0)
    lane = lax.broadcasted_iota(jnp.int32, (rows, columns), 1)
    return jnp.where((lane >> 6) == row, 1.0, 0.0).astype(BF16)


def gather_matrix(rows, columns):
    row = lax.broadcasted_iota(jnp.int32, (rows, columns), 0)
    lane = lax.broadcasted_iota(jnp.int32, (rows, columns), 1)
    return jnp.where((row >> 6) == lane, 1.0, 0.0).astype(BF16)


def softplus(value):
    small = jnp.exp(-jnp.abs(value))
    series = small * (1.0 - small * (0.5 - small * (1.0 / 3.0 - small * 0.25)))
    return jnp.maximum(value, 0.0) + jnp.where(small < 0.01, series, jnp.log(1.0 + small))


def block_marks(flags):
    row = lax.broadcasted_iota(jnp.int32, (BLOCK, BLOCK), 0)
    lane = lax.broadcasted_iota(jnp.int32, (BLOCK, BLOCK), 1)
    lower = jnp.where(row >= lane, 1.0, 0.0)
    upper = jnp.where(row <= lane, 1.0, 0.0)
    seg_col = jnp.sum(lower * flags, axis=1, keepdims=True)
    seg_row = mm(jnp.broadcast_to(flags, (8, BLOCK)).astype(BF16), upper.astype(BF16))[0:1]
    last = jnp.sum(flags, axis=1, keepdims=True)
    mask = jnp.where(seg_col == seg_row, lower, 0.0)
    alive = jnp.where(seg_col == 0.0, 1.0, 0.0)
    tail = jnp.where(seg_col == last, 1.0, 0.0)
    alive_last = jnp.where(last == 0.0, 1.0, 0.0)
    return mask, alive, tail, alive_last


def head_steps(raw, bias, power, length):
    rate = -0.5 * jnp.exp((power.astype(F32) / 3.0 - 1.0) * math.log(length))
    step = softplus(raw + bias)
    return step, rate


def block_scales(step, rate):
    row = lax.broadcasted_iota(jnp.int32, (BLOCK, BLOCK), 0)
    lane = lax.broadcasted_iota(jnp.int32, (BLOCK, BLOCK), 1)
    lower = jnp.where(row >= lane, 1.0, 0.0).astype(BF16)
    cum = exact_left(lower, step * rate, 3)
    total = cum[BLOCK - 1 : BLOCK]
    middle = 0.5 * total
    return jnp.exp(cum - middle), step * jnp.exp(middle - cum), jnp.exp(middle), jnp.exp(total)


def front_kernel(
    length, input_ref, rim_ref, raw_ref, flags_ref, power_ref, weight_ref, bias_ref, step_bias_ref, grad_ref,
    act_ref, slope_ref, bx_ref, ady_ref, pack_ref, padded,
):
    tokens, channels = input_ref.shape
    heads = raw_ref.shape[1]
    inner = heads * HEAD_WIDTH
    padded[0:8, :] = jnp.zeros((8, channels), F32)
    padded[8 - (KERNEL - 1) : 8, :] = rim_ref[...].astype(F32)
    padded[8 : 8 + tokens, :] = input_ref[...].astype(F32)
    weight = weight_ref[...].astype(F32)
    for low in range(0, channels, 128):
        cols = slice(low, low + 128)
        for start in range(0, tokens, 64):
            total = jnp.broadcast_to(bias_ref[:, cols], (64, 128))
            for tap in range(KERNEL):
                at = 8 - (KERNEL - 1) + start + tap
                total = total + padded[at : at + 64, cols] * weight[tap : tap + 1, cols]
            gate = 1.0 / (1.0 + jnp.exp(-total))
            act_ref[start : start + 64, cols] = (total * gate).astype(BF16)
            slope_ref[start : start + 64, cols] = gate * (1.0 + total * (1.0 - gate))

    step, rate = head_steps(raw_ref[...], step_bias_ref[...], power_ref[...], length)
    spread = spread_matrix(heads, inner)
    flags = flags_ref[...].astype(F32)
    blocks = tokens // BLOCK
    fresh, back, passing = [], [], []
    passing_heads = jnp.ones((1, heads), F32)
    for block in range(blocks):
        rows = slice(block * BLOCK, (block + 1) * BLOCK)
        _, alive, tail, alive_last = block_marks(flags[block : block + 1])
        row_scale, col_scale, half, whole = block_scales(step[rows], rate)
        through = whole * alive_last
        passing_heads = passing_heads * through
        line = lax.broadcasted_iota(jnp.int32, (8, heads), 0)
        both = exact_right(jnp.where(line == 0, half, through), spread, 3)
        half_wide, through_wide = both[0:1], both[1:2]
        bx = (act_ref[rows, 0:inner].astype(F32) * exact_right(col_scale, spread, 2)).astype(BF16)
        ady = (grad_ref[rows, :].astype(F32) * exact_right(row_scale, spread, 2)).astype(BF16)
        bx_ref[rows, :] = bx
        ady_ref[rows, :] = ady
        keys = (act_ref[rows, inner : inner + STATE].astype(F32) * tail).astype(BF16)
        queries = (act_ref[rows, inner + STATE : inner + 2 * STATE].astype(F32) * alive).astype(BF16)
        fresh.append(mm_tn(keys, bx) * half_wide)
        back.append(mm_tn(queries, ady) * half_wide)
        passing.append(through_wide)
    up = fresh[0]
    for block in range(1, blocks):
        up = passing[block] * up + fresh[block]
    down = back[blocks - 1]
    for block in range(blocks - 2, -1, -1):
        down = passing[block] * down + back[block]
    chunks = STATE // ROWS
    pack_ref[:, :, 0:inner] = jnp.concatenate(
        [up.reshape(chunks, ROWS, inner), down.reshape(chunks, ROWS, inner)], axis=1
    ).astype(BF16)
    hi, mid, lo = [piece.astype(F32) for piece in pieces_of(passing_heads, 3)]
    line = lax.broadcasted_iota(jnp.int32, (2 * ROWS, heads), 0)
    stack = jnp.where(line == 0, hi, jnp.where(line == 1, mid, jnp.where(line == 2, lo, 0.0)))
    row = lax.broadcasted_iota(jnp.int32, (heads, EXTRA), 0)
    lane = lax.broadcasted_iota(jnp.int32, (heads, EXTRA), 1)
    wide = mm(stack.astype(BF16), jnp.where(row == lane, 1.0, 0.0).astype(BF16))
    pack_ref[:, :, inner : inner + EXTRA] = jnp.broadcast_to(wide[None], (chunks, 2 * ROWS, EXTRA)).astype(BF16)


def scan_kernel(pack_ref, out_ref):
    devices, _, width = pack_ref.shape
    inner = width - EXTRA
    spread = spread_matrix(EXTRA, inner)
    passing = []
    for device in range(devices):
        passing.append(jnp.sum(mm(pack_ref[device, :, inner:width], spread), axis=0, keepdims=True))
    before, after = [None] * devices, [None] * devices
    up = jnp.zeros((ROWS, inner), F32)
    down = jnp.zeros((ROWS, inner), F32)
    for device in range(devices):
        before[device] = up
        up = passing[device] * up + pack_ref[device, :, 0:inner].astype(F32)[0:ROWS]
    for device in range(devices - 1, -1, -1):
        after[device] = down
        down = passing[device] * down + pack_ref[device, :, 0:inner].astype(F32)[ROWS : 2 * ROWS]
    for device in range(devices):
        out_ref[device] = jnp.concatenate([before[device], after[device]], axis=0).astype(BF16)


def back_kernel(
    length, carry_ref, act_ref, slope_ref, bx_ref, ady_ref, grad_ref, input_ref, rim_ref, raw_ref, flags_ref,
    power_ref, weight_ref, step_bias_ref, skip_ref,
    out_ref, edge_ref, head_ref, raw_out_ref, sums_ref, padded, dpre,
):
    tokens, channels = input_ref.shape
    heads = raw_ref.shape[1]
    inner = heads * HEAD_WIDTH
    blocks = tokens // BLOCK
    raw = raw_ref[...]
    step, rate = head_steps(raw, step_bias_ref[...], power_ref[...], length)
    spread = spread_matrix(heads, inner)
    gather = gather_matrix(inner, heads)
    flags = flags_ref[...].astype(F32)
    carry = carry_ref[...].astype(F32)
    entering = carry[:, 0:ROWS].reshape(STATE, inner)
    leaving = carry[:, ROWS : 2 * ROWS].reshape(STATE, inner)
    skip_wide = exact_right(jnp.broadcast_to(skip_ref[...], (8, heads)), spread, 3)[0:1]

    marks, scales, keys, queries, fresh, back, halves, throughs = [], [], [], [], [], [], [], []
    for block in range(blocks):
        rows = slice(block * BLOCK, (block + 1) * BLOCK)
        mark = block_marks(flags[block : block + 1])
        scale = block_scales(step[rows], rate)
        marks.append(mark)
        scales.append(scale)
        line = lax.broadcasted_iota(jnp.int32, (8, heads), 0)
        both = exact_right(jnp.where(line == 0, scale[2], scale[3] * mark[3]), spread, 3)
        halves.append(both[0:1])
        throughs.append(both[1:2])
        keys.append((act_ref[rows, inner : inner + STATE].astype(F32) * mark[2]).astype(BF16))
        queries.append((act_ref[rows, inner + STATE : inner + 2 * STATE].astype(F32) * mark[1]).astype(BF16))
        fresh.append(mm_tn(keys[block], bx_ref[rows, :]))
        back.append(mm_tn(queries[block], ady_ref[rows, :]))
    states = [entering]
    for block in range(blocks - 1):
        states.append(throughs[block] * states[block] + halves[block] * fresh[block])
    grads = [None] * blocks
    grads[blocks - 1] = leaving
    for block in range(blocks - 1, 0, -1):
        grads[block - 1] = throughs[block] * grads[block] + halves[block] * back[block]

    row = lax.broadcasted_iota(jnp.int32, (BLOCK, BLOCK), 0)
    lane = lax.broadcasted_iota(jnp.int32, (BLOCK, BLOCK), 1)
    upper = jnp.where(row <= lane, 1.0, 0.0).astype(BF16)
    at_last = jnp.where(lax.broadcasted_iota(jnp.int32, (BLOCK, heads), 0) == BLOCK - 1, 1.0, 0.0)
    for block in range(blocks):
        rows = slice(block * BLOCK, (block + 1) * BLOCK)
        mask, alive, tail, alive_last = marks[block]
        state = (halves[block] * states[block]).astype(BF16)
        grad = (halves[block] * grads[block]).astype(BF16)
        bx = bx_ref[rows, :]
        ady = ady_ref[rows, :]
        key = act_ref[rows, inner : inner + STATE]
        query = act_ref[rows, inner + STATE : inner + 2 * STATE]
        scores = mask * mm_nt(query, key)
        scores_t = scores.T.astype(BF16)
        scores = scores.astype(BF16)
        result = mm(scores, bx) + mm(queries[block], state)
        row_sum = exact_right(ady.astype(F32) * result, gather, 2)
        dbx = mm(scores_t, ady) + mm(keys[block], grad)
        col_sum = exact_right(bx.astype(F32) * dbx, gather, 2)
        dscores = mask * mm_nt(ady, bx)
        dscores_t = dscores.T.astype(BF16)
        dquery = mm(dscores.astype(BF16), key) + alive * mm_nt(ady, state)
        dkey = mm(dscores_t, query) + tail * mm_nt(bx, grad)
        whole = jnp.sum(
            grad.astype(F32) * fresh[block] + throughs[block] * (grads[block] * states[block]), axis=0, keepdims=True
        )
        whole = exact_right(jnp.broadcast_to(whole, (8, inner)), gather, 3)[0:1]
        dlog = exact_left(upper, row_sum - col_sum + at_last * whole, 3)
        dstep = col_sum / step[rows] + rate * dlog
        raw_out_ref[rows, :] = dstep / (1.0 + jnp.exp(-(raw[rows] + step_bias_ref[...])))
        dx = exact_right(scales[block][1], spread, 2) * dbx + skip_wide * grad_ref[rows, :].astype(F32)
        dpre[rows, 0:inner] = dx * slope_ref[rows, 0:inner]
        dpre[rows, inner : inner + STATE] = dkey * slope_ref[rows, inner : inner + STATE]
        dpre[rows, inner + STATE : channels] = dquery * slope_ref[rows, inner + STATE : channels]

    dpre[tokens : tokens + 8, :] = jnp.zeros((8, channels), F32)
    padded[0:8, :] = jnp.zeros((8, channels), F32)
    padded[8 - (KERNEL - 1) : 8, :] = rim_ref[...].astype(F32)
    padded[8 : 8 + tokens, :] = input_ref[...].astype(F32)
    weight = weight_ref[...].astype(F32)
    for low in range(0, channels, 128):
        cols = slice(low, low + 128)
        acc = [jnp.zeros((8, 128), F32) for _ in range(KERNEL + 1)]
        for start in range(0, tokens, 64):
            here = dpre[start : start + 64, cols]
            total = here * weight[KERNEL - 1 : KERNEL, cols]
            for tap in range(KERNEL - 1):
                ahead = start + KERNEL - 1 - tap
                total = total + dpre[ahead : ahead + 64, cols] * weight[tap : tap + 1, cols]
            out_ref[start : start + 64, cols] = total.astype(BF16)
            if start == tokens - 64:
                edge_ref[:, cols] = total[48:64]
            for tap in range(KERNEL):
                at = 8 - (KERNEL - 1) + start + tap
                acc[tap] = acc[tap] + jnp.sum((here * padded[at : at + 64, cols]).reshape(8, 8, 128), axis=0)
            acc[KERNEL] = acc[KERNEL] + jnp.sum(here.reshape(8, 8, 128), axis=0)
        line = lax.broadcasted_iota(jnp.int32, (8, 128), 0)
        block_sums = jnp.zeros((8, 128), F32)
        for tap in range(KERNEL + 1):
            block_sums = jnp.where(line == tap, jnp.sum(acc[tap], axis=0, keepdims=True), block_sums)
        sums_ref[:, cols] = block_sums
        first = [dpre[at : at + 1, cols] for at in range(KERNEL - 1)]
        lines = jnp.zeros((8, 128), F32)
        for at in range(KERNEL - 1):
            part = sum(weight[tap : tap + 1, cols] * first[at - tap] for tap in range(at + 1))
            lines = jnp.where(line == at, part, lines)
        head_ref[:, cols] = lines


def call(kernel, out_shape, scratch=(), flops=0, moved=0):
    return pl.pallas_call(
        kernel,
        out_shape=out_shape,
        scratch_shapes=list(scratch),
        compiler_params=pltpu.CompilerParams(vmem_limit_bytes=VMEM_BYTES),
        cost_estimate=pl.CostEstimate(flops=flops, bytes_accessed=moved, transcendentals=0),
    )


def shifted(value, axis, by):
    devices = lax.axis_size(axis)
    pairs = [(i, i + by) for i in range(devices) if 0 <= i + by < devices]
    return lax.ppermute(value, axis, pairs)


def body(
    conv_input, step_raw, doc_starts, decay_power, conv_weight, conv_bias, step_bias, skip_gain, grad_out
):
    tokens, channels = conv_input.shape[1:]
    heads = step_raw.shape[2]
    inner = heads * HEAD_WIDTH
    ctx_size = lax.axis_size("ctx")
    dp_size = lax.axis_size("dp")
    length = tokens * ctx_size
    chunks = STATE // ROWS
    inputs = conv_input[0]
    rim = shifted(inputs[tokens - (KERNEL - 1) :], "ctx", 1)
    raw = step_raw[0]
    flags = doc_starts.reshape(tokens // BLOCK, BLOCK)
    power = decay_power[None]
    step_bias = step_bias[None]
    skip = skip_gain[None]
    grads = grad_out[0]
    shape = jax.ShapeDtypeStruct

    act, slope, bx, ady, pack = call(
        lambda *refs: front_kernel(length, *refs),
        (
            shape((tokens, channels), BF16),
            shape((tokens, channels), F32),
            shape((tokens, inner), BF16),
            shape((tokens, inner), BF16),
            shape((chunks, 2 * ROWS, inner + EXTRA), BF16),
        ),
        [pltpu.VMEM((tokens + 8, channels), F32)],
    )(inputs, rim, raw, flags, power, conv_weight, conv_bias[None], step_bias, grads)

    gathered = lax.all_to_all(pack, "ctx", 0, 0, tiled=True)
    scanned = call(scan_kernel, shape((ctx_size, 2 * ROWS, inner), BF16))(gathered)
    carry = lax.all_to_all(scanned, "ctx", 0, 0, tiled=True)

    out, edge, head, grad_raw, sums = call(
        lambda *refs: back_kernel(length, *refs),
        (
            shape((tokens, channels), BF16),
            shape((16, channels), F32),
            shape((8, channels), F32),
            shape((tokens, heads), F32),
            shape((8, channels), F32),
        ),
        [pltpu.VMEM((tokens + 8, channels), F32), pltpu.VMEM((tokens + 8, channels), F32)],
    )(carry, act, slope, bx, ady, grads, inputs, rim, raw, flags, power, conv_weight, step_bias, skip)

    devices = dp_size * ctx_size
    width = channels // devices
    terms = sums[: KERNEL + 1].reshape(KERNEL + 1, devices, width).transpose(1, 0, 2)
    shard = jnp.sum(lax.all_to_all(terms, ("dp", "ctx"), 0, 0, tiled=True), axis=0)
    shard = shard * (1.0 / (dp_size * length))
    back = shifted(head[: KERNEL - 1], "ctx", -1)
    edge = jnp.concatenate([edge[: 16 - (KERNEL - 1)], edge[16 - (KERNEL - 1) :] + back], 0)
    grad_input = lax.dynamic_update_slice(out, edge.astype(BF16), (tokens - 16, 0))
    return (grad_input[None], grad_raw[None], shard[:KERNEL][:, None, :], shard[KERNEL][None, :])


def solution(mesh):
    return jax.shard_map(
        body,
        mesh=mesh,
        in_specs=(
            P("dp", "ctx", "tp"),
            P("dp", "ctx", "tp"),
            P("dp", "ctx"),
            P("tp"),
            P(None, "tp"),
            P("tp"),
            P("tp"),
            P("tp"),
            P("dp", "ctx", "tp"),
        ),
        out_specs=(
            P("dp", "ctx", "tp"),
            P("dp", "ctx", "tp"),
            P(None, "tp", ("dp", "ctx")),
            P("tp", ("dp", "ctx")),
        ),
        check_vma=False,
    )
```

```python
import math

import jax
import jax.numpy as jnp
from jax import lax
from jax.experimental import pallas as pl
from jax.experimental.pallas import tpu as pltpu
from jax.sharding import PartitionSpec as P

BLOCK = 128
HEAD_WIDTH = 64
STATE = 128
KERNEL = 4
SPLIT = 4
ROWS = STATE // SPLIT
EXTRA = 128
VMEM_BYTES = 50 * 1024 * 1024
F32 = jnp.float32
BF16 = jnp.bfloat16
CTX = ("ch", "cl")


def mm(left, right):
    return jnp.dot(left, right, preferred_element_type=F32)


def mm_nt(left, right):
    return lax.dot_general(left, right, (((1,), (1,)), ((), ())), preferred_element_type=F32)


def mm_tn(left, right):
    return lax.dot_general(left, right, (((0,), (0,)), ((), ())), preferred_element_type=F32)


def pieces_of(value, count):
    out = []
    for _ in range(count):
        piece = value.astype(BF16)
        out.append(piece)
        value = value - piece.astype(F32)
    return out


def exact_left(ones, value, count):
    return sum(mm(ones, piece) for piece in pieces_of(value, count))


def exact_right(value, ones, count):
    return sum(mm(piece, ones) for piece in pieces_of(value, count))


def spread_matrix(rows, columns):
    row = lax.broadcasted_iota(jnp.int32, (rows, columns), 0)
    lane = lax.broadcasted_iota(jnp.int32, (rows, columns), 1)
    return jnp.where((lane >> 6) == row, 1.0, 0.0).astype(BF16)


def gather_matrix(rows, columns):
    row = lax.broadcasted_iota(jnp.int32, (rows, columns), 0)
    lane = lax.broadcasted_iota(jnp.int32, (rows, columns), 1)
    return jnp.where((row >> 6) == lane, 1.0, 0.0).astype(BF16)


def softplus(value):
    small = jnp.exp(-jnp.abs(value))
    series = small * (1.0 - small * (0.5 - small * (1.0 / 3.0 - small * 0.25)))
    return jnp.maximum(value, 0.0) + jnp.where(small < 0.01, series, jnp.log(1.0 + small))


def block_marks(flags):
    row = lax.broadcasted_iota(jnp.int32, (BLOCK, BLOCK), 0)
    lane = lax.broadcasted_iota(jnp.int32, (BLOCK, BLOCK), 1)
    lower = jnp.where(row >= lane, 1.0, 0.0)
    upper = jnp.where(row <= lane, 1.0, 0.0)
    seg_col = jnp.sum(lower * flags, axis=1, keepdims=True)
    seg_row = mm(jnp.broadcast_to(flags, (8, BLOCK)).astype(BF16), upper.astype(BF16))[0:1]
    last = jnp.sum(flags, axis=1, keepdims=True)
    mask = jnp.where(seg_col == seg_row, lower, 0.0)
    alive = jnp.where(seg_col == 0.0, 1.0, 0.0)
    tail = jnp.where(seg_col == last, 1.0, 0.0)
    alive_last = jnp.where(last == 0.0, 1.0, 0.0)
    return mask, alive, tail, alive_last


def head_steps(raw, bias, power, length):
    rate = -0.5 * jnp.exp((power.astype(F32) / 3.0 - 1.0) * math.log(length))
    step = softplus(raw + bias)
    return step, rate


def block_scales(step, rate):
    row = lax.broadcasted_iota(jnp.int32, (BLOCK, BLOCK), 0)
    lane = lax.broadcasted_iota(jnp.int32, (BLOCK, BLOCK), 1)
    lower = jnp.where(row >= lane, 1.0, 0.0).astype(BF16)
    cum = exact_left(lower, step * rate, 3)
    total = cum[BLOCK - 1 : BLOCK]
    middle = 0.5 * total
    return jnp.exp(cum - middle), step * jnp.exp(middle - cum), jnp.exp(middle), jnp.exp(total)


def front_kernel(
    length, input_ref, rim_ref, raw_ref, flags_ref, power_ref, weight_ref, bias_ref, step_bias_ref, grad_ref,
    act_ref, slope_ref, bx_ref, ady_ref, pack_ref, padded,
):
    tokens, channels = input_ref.shape
    heads = raw_ref.shape[1]
    inner = heads * HEAD_WIDTH
    padded[0:8, :] = jnp.zeros((8, channels), F32)
    padded[8 - (KERNEL - 1) : 8, :] = rim_ref[...].astype(F32)
    padded[8 : 8 + tokens, :] = input_ref[...].astype(F32)
    weight = weight_ref[...].astype(F32)
    for low in range(0, channels, 128):
        cols = slice(low, low + 128)
        for start in range(0, tokens, 64):
            total = jnp.broadcast_to(bias_ref[:, cols], (64, 128))
            for tap in range(KERNEL):
                at = 8 - (KERNEL - 1) + start + tap
                total = total + padded[at : at + 64, cols] * weight[tap : tap + 1, cols]
            gate = 1.0 / (1.0 + jnp.exp(-total))
            act_ref[start : start + 64, cols] = (total * gate).astype(BF16)
            slope_ref[start : start + 64, cols] = gate * (1.0 + total * (1.0 - gate))

    step, rate = head_steps(raw_ref[...], step_bias_ref[...], power_ref[...], length)
    spread = spread_matrix(heads, inner)
    flags = flags_ref[...].astype(F32)
    blocks = tokens // BLOCK
    fresh, back, passing = [], [], []
    passing_heads = jnp.ones((1, heads), F32)
    for block in range(blocks):
        rows = slice(block * BLOCK, (block + 1) * BLOCK)
        _, alive, tail, alive_last = block_marks(flags[block : block + 1])
        row_scale, col_scale, half, whole = block_scales(step[rows], rate)
        through = whole * alive_last
        passing_heads = passing_heads * through
        line = lax.broadcasted_iota(jnp.int32, (8, heads), 0)
        both = exact_right(jnp.where(line == 0, half, through), spread, 3)
        half_wide, through_wide = both[0:1], both[1:2]
        bx = (act_ref[rows, 0:inner].astype(F32) * exact_right(col_scale, spread, 2)).astype(BF16)
        ady = (grad_ref[rows, :].astype(F32) * exact_right(row_scale, spread, 2)).astype(BF16)
        bx_ref[rows, :] = bx
        ady_ref[rows, :] = ady
        keys = (act_ref[rows, inner : inner + STATE].astype(F32) * tail).astype(BF16)
        queries = (act_ref[rows, inner + STATE : inner + 2 * STATE].astype(F32) * alive).astype(BF16)
        fresh.append(mm_tn(keys, bx) * half_wide)
        back.append(mm_tn(queries, ady) * half_wide)
        passing.append(through_wide)
    up = fresh[0]
    for block in range(1, blocks):
        up = passing[block] * up + fresh[block]
    down = back[blocks - 1]
    for block in range(blocks - 2, -1, -1):
        down = passing[block] * down + back[block]
    pack_ref[:, :, 0:inner] = jnp.concatenate(
        [up.reshape(SPLIT, ROWS, inner), down.reshape(SPLIT, ROWS, inner)], axis=1
    ).astype(BF16)
    row = lax.broadcasted_iota(jnp.int32, (heads, EXTRA), 0)
    lane = lax.broadcasted_iota(jnp.int32, (heads, EXTRA), 1)
    place = jnp.where(row == lane, 1.0, 0.0).astype(BF16)
    wide = exact_right(jnp.broadcast_to(passing_heads, (8, heads)), place, 3)[0:1]
    pack_ref[:, :, inner : inner + EXTRA] = jnp.broadcast_to(
        stacked(wide, 2 * ROWS)[None], (SPLIT, 2 * ROWS, EXTRA)
    )


def stacked(value, rows):
    hi, mid, lo = [piece.astype(F32) for piece in pieces_of(value, 3)]
    line = lax.broadcasted_iota(jnp.int32, (rows, EXTRA), 0)
    return jnp.where(line == 0, hi, jnp.where(line == 1, mid, jnp.where(line == 2, lo, 0.0))).astype(BF16)


def passed(pack_ref, source, inner, spread):
    lines = pack_ref[source, 0:16, inner : inner + EXTRA]
    return (
        jnp.sum(lines.astype(F32), axis=0, keepdims=True),
        jnp.sum(mm(lines, spread), axis=0, keepdims=True),
    )


def totals_kernel(near_ref, out_ref):
    inner = near_ref.shape[2] - EXTRA
    group = lax.axis_index("ch")
    spread = spread_matrix(EXTRA, inner)
    decay = [passed(near_ref, source, inner, spread) for source in range(SPLIT)]
    up = jnp.zeros((ROWS, inner), F32)
    down = jnp.zeros((ROWS, inner), F32)
    through = jnp.ones((1, EXTRA), F32)
    for source in range(SPLIT):
        up = decay[source][1] * up + near_ref[source, 0:ROWS, 0:inner].astype(F32)
        through = through * decay[source][0]
    for source in range(SPLIT - 1, -1, -1):
        down = decay[source][1] * down + near_ref[source, ROWS : 2 * ROWS, 0:inner].astype(F32)
    lines = stacked(through, ROWS)
    for target in range(SPLIT):
        later = jnp.where(target > group, 1.0, 0.0)
        out_ref[target, :, 0:inner] = (later * up + (1.0 - later) * down).astype(BF16)
        out_ref[target, :, inner : inner + EXTRA] = lines


def states_kernel(near_ref, far_ref, out_ref):
    inner = near_ref.shape[2] - EXTRA
    group = lax.axis_index("ch")
    spread = spread_matrix(EXTRA, inner)
    near = [passed(near_ref, source, inner, spread)[1] for source in range(SPLIT)]
    far = [passed(far_ref, source, inner, spread)[1] for source in range(SPLIT)]
    up = jnp.zeros((ROWS, inner), F32)
    down = jnp.zeros((ROWS, inner), F32)
    for source in range(SPLIT):
        use = jnp.where(source < group, 1.0, 0.0)
        up = (use * far[source] + (1.0 - use)) * up + use * far_ref[source, :, 0:inner].astype(F32)
    for source in range(SPLIT - 1, -1, -1):
        use = jnp.where(source > group, 1.0, 0.0)
        down = (use * far[source] + (1.0 - use)) * down + use * far_ref[source, :, 0:inner].astype(F32)
    for source in range(SPLIT):
        out_ref[source, 0:ROWS, :] = up.astype(BF16)
        up = near[source] * up + near_ref[source, 0:ROWS, 0:inner].astype(F32)
    for source in range(SPLIT - 1, -1, -1):
        out_ref[source, ROWS : 2 * ROWS, :] = down.astype(BF16)
        down = near[source] * down + near_ref[source, ROWS : 2 * ROWS, 0:inner].astype(F32)


def back_kernel(
    length, carry_ref, act_ref, slope_ref, bx_ref, ady_ref, grad_ref, input_ref, rim_ref, raw_ref, flags_ref,
    power_ref, weight_ref, step_bias_ref, skip_ref,
    out_ref, edge_ref, head_ref, raw_out_ref, terms_ref, padded, dpre, sums_ref,
):
    tokens, channels = input_ref.shape
    heads = raw_ref.shape[1]
    inner = heads * HEAD_WIDTH
    blocks = tokens // BLOCK
    raw = raw_ref[...]
    step, rate = head_steps(raw, step_bias_ref[...], power_ref[...], length)
    spread = spread_matrix(heads, inner)
    gather = gather_matrix(inner, heads)
    flags = flags_ref[...].astype(F32)
    carry = carry_ref[...].astype(F32)
    entering = carry[:, 0:ROWS].reshape(STATE, inner)
    leaving = carry[:, ROWS : 2 * ROWS].reshape(STATE, inner)
    skip_wide = exact_right(jnp.broadcast_to(skip_ref[...], (8, heads)), spread, 3)[0:1]

    marks, scales, keys, queries, fresh, back, halves, throughs = [], [], [], [], [], [], [], []
    for block in range(blocks):
        rows = slice(block * BLOCK, (block + 1) * BLOCK)
        mark = block_marks(flags[block : block + 1])
        scale = block_scales(step[rows], rate)
        marks.append(mark)
        scales.append(scale)
        line = lax.broadcasted_iota(jnp.int32, (8, heads), 0)
        both = exact_right(jnp.where(line == 0, scale[2], scale[3] * mark[3]), spread, 3)
        halves.append(both[0:1])
        throughs.append(both[1:2])
        keys.append((act_ref[rows, inner : inner + STATE].astype(F32) * mark[2]).astype(BF16))
        queries.append((act_ref[rows, inner + STATE : inner + 2 * STATE].astype(F32) * mark[1]).astype(BF16))
        fresh.append(mm_tn(keys[block], bx_ref[rows, :]))
        back.append(mm_tn(queries[block], ady_ref[rows, :]))
    states = [entering]
    for block in range(blocks - 1):
        states.append(throughs[block] * states[block] + halves[block] * fresh[block])
    grads = [None] * blocks
    grads[blocks - 1] = leaving
    for block in range(blocks - 1, 0, -1):
        grads[block - 1] = throughs[block] * grads[block] + halves[block] * back[block]

    row = lax.broadcasted_iota(jnp.int32, (BLOCK, BLOCK), 0)
    lane = lax.broadcasted_iota(jnp.int32, (BLOCK, BLOCK), 1)
    upper = jnp.where(row <= lane, 1.0, 0.0).astype(BF16)
    at_last = jnp.where(lax.broadcasted_iota(jnp.int32, (BLOCK, heads), 0) == BLOCK - 1, 1.0, 0.0)
    for block in range(blocks):
        rows = slice(block * BLOCK, (block + 1) * BLOCK)
        mask, alive, tail, alive_last = marks[block]
        state = (halves[block] * states[block]).astype(BF16)
        grad = (halves[block] * grads[block]).astype(BF16)
        bx = bx_ref[rows, :]
        ady = ady_ref[rows, :]
        key = act_ref[rows, inner : inner + STATE]
        query = act_ref[rows, inner + STATE : inner + 2 * STATE]
        scores = mask * mm_nt(query, key)
        scores_t = scores.T.astype(BF16)
        scores = scores.astype(BF16)
        result = mm(scores, bx) + mm(queries[block], state)
        row_sum = exact_right(ady.astype(F32) * result, gather, 2)
        dbx = mm(scores_t, ady) + mm(keys[block], grad)
        col_sum = exact_right(bx.astype(F32) * dbx, gather, 2)
        dscores = mask * mm_nt(ady, bx)
        dscores_t = dscores.T.astype(BF16)
        dquery = mm(dscores.astype(BF16), key) + alive * mm_nt(ady, state)
        dkey = mm(dscores_t, query) + tail * mm_nt(bx, grad)
        whole = jnp.sum(
            grad.astype(F32) * fresh[block] + throughs[block] * (grads[block] * states[block]), axis=0, keepdims=True
        )
        whole = exact_right(jnp.broadcast_to(whole, (8, inner)), gather, 3)[0:1]
        dlog = exact_left(upper, row_sum - col_sum + at_last * whole, 3)
        dstep = col_sum / step[rows] + rate * dlog
        raw_out_ref[rows, :] = dstep / (1.0 + jnp.exp(-(raw[rows] + step_bias_ref[...])))
        dx = exact_right(scales[block][1], spread, 2) * dbx + skip_wide * grad_ref[rows, :].astype(F32)
        dpre[rows, 0:inner] = dx * slope_ref[rows, 0:inner]
        dpre[rows, inner : inner + STATE] = dkey * slope_ref[rows, inner : inner + STATE]
        dpre[rows, inner + STATE : channels] = dquery * slope_ref[rows, inner + STATE : channels]

    dpre[tokens : tokens + 8, :] = jnp.zeros((8, channels), F32)
    padded[0:8, :] = jnp.zeros((8, channels), F32)
    padded[8 - (KERNEL - 1) : 8, :] = rim_ref[...].astype(F32)
    padded[8 : 8 + tokens, :] = input_ref[...].astype(F32)
    weight = weight_ref[...].astype(F32)
    for low in range(0, channels, 128):
        cols = slice(low, low + 128)
        acc = [jnp.zeros((8, 128), F32) for _ in range(KERNEL + 1)]
        for start in range(0, tokens, 64):
            here = dpre[start : start + 64, cols]
            total = here * weight[KERNEL - 1 : KERNEL, cols]
            for tap in range(KERNEL - 1):
                ahead = start + KERNEL - 1 - tap
                total = total + dpre[ahead : ahead + 64, cols] * weight[tap : tap + 1, cols]
            out_ref[start : start + 64, cols] = total.astype(BF16)
            if start == tokens - 64:
                edge_ref[:, cols] = total[48:64]
            for tap in range(KERNEL):
                at = 8 - (KERNEL - 1) + start + tap
                acc[tap] = acc[tap] + jnp.sum((here * padded[at : at + 64, cols]).reshape(8, 8, 128), axis=0)
            acc[KERNEL] = acc[KERNEL] + jnp.sum(here.reshape(8, 8, 128), axis=0)
        line = lax.broadcasted_iota(jnp.int32, (8, 128), 0)
        block_sums = jnp.zeros((8, 128), F32)
        for tap in range(KERNEL + 1):
            block_sums = jnp.where(line == tap, jnp.sum(acc[tap], axis=0, keepdims=True), block_sums)
        sums_ref[:, cols] = block_sums
        first = [dpre[at : at + 1, cols] for at in range(KERNEL - 1)]
        lines = jnp.zeros((8, 128), F32)
        for at in range(KERNEL - 1):
            part = sum(weight[tap : tap + 1, cols] * first[at - tap] for tap in range(at + 1))
            lines = jnp.where(line == at, part, lines)
        head_ref[:, cols] = lines

    targets = terms_ref.shape[0]
    width = channels // targets
    line = lax.broadcasted_iota(jnp.int32, (8, 128), 0)
    lane = lax.broadcasted_iota(jnp.int32, (8, 128), 1)
    own = (lane >= line * width) & (lane < (line + 1) * width) & (line <= KERNEL)
    for tile in range(channels // 128, sums_ref.shape[1] // 128):
        sums_ref[:, tile * 128 : tile * 128 + 128] = jnp.zeros((8, 128), F32)
    aside = pltpu.roll(sums_ref[...], 0, 1, stride=width // 2, stride_axis=0)
    sums_ref[...] = pltpu.roll(aside, 0, 1, stride=width - width // 2, stride_axis=0)
    for target in range(targets):
        tile, at = divmod(target * width, 128)
        part = sums_ref[:, tile * 128 : tile * 128 + 128]
        if at:
            part = jnp.where(lane >= at, part, sums_ref[:, tile * 128 + 128 : tile * 128 + 256])
            part = pltpu.roll(part, 128 - at, 1)
        terms_ref[target : target + 1, :] = jnp.sum(jnp.where(own, part, 0.0), axis=0, keepdims=True)


def call(kernel, out_shape, scratch=(), flops=0, moved=0):
    return pl.pallas_call(
        kernel,
        out_shape=out_shape,
        scratch_shapes=list(scratch),
        compiler_params=pltpu.CompilerParams(vmem_limit_bytes=VMEM_BYTES),
        cost_estimate=pl.CostEstimate(flops=flops, bytes_accessed=moved, transcendentals=0),
    )


def shifted(value, axis, by):
    devices = lax.axis_size(axis)
    pairs = [(i, i + by) for i in range(devices) if 0 <= i + by < devices]
    return lax.ppermute(value, axis, pairs)


def body(
    conv_input, step_raw, doc_starts, decay_power, conv_weight, conv_bias, step_bias, skip_gain, grad_out
):
    tokens, channels = conv_input.shape[1:]
    heads = step_raw.shape[2]
    inner = heads * HEAD_WIDTH
    ctx_size = lax.axis_size(CTX)
    dp_size = lax.axis_size("dp")
    devices = dp_size * ctx_size
    length = tokens * ctx_size
    inputs = conv_input[0]
    rim = shifted(inputs[tokens - (KERNEL - 1) :], CTX, 1)
    raw = step_raw[0]
    flags = doc_starts.reshape(tokens // BLOCK, BLOCK)
    power = decay_power[None]
    step_bias = step_bias[None]
    skip = skip_gain[None]
    grads = grad_out[0]
    shape = jax.ShapeDtypeStruct

    act, slope, bx, ady, pack = call(
        lambda *refs: front_kernel(length, *refs),
        (
            shape((tokens, channels), BF16),
            shape((tokens, channels), F32),
            shape((tokens, inner), BF16),
            shape((tokens, inner), BF16),
            shape((SPLIT, 2 * ROWS, inner + EXTRA), BF16),
        ),
        [pltpu.VMEM((tokens + 8, channels), F32)],
    )(inputs, rim, raw, flags, power, conv_weight, conv_bias[None], step_bias, grads)

    near = lax.all_to_all(pack, "cl", 0, 0, tiled=True)
    totals = call(totals_kernel, shape((SPLIT, ROWS, inner + EXTRA), BF16))(near)
    far = lax.all_to_all(totals, "ch", 0, 0, tiled=True)
    states = call(states_kernel, shape((SPLIT, 2 * ROWS, inner), BF16))(near, far)
    carry = lax.all_to_all(states, "cl", 0, 0, tiled=True)

    out, edge, head, grad_raw, terms = call(
        lambda *refs: back_kernel(length, *refs),
        (
            shape((tokens, channels), BF16),
            shape((16, channels), F32),
            shape((8, channels), F32),
            shape((tokens, heads), F32),
            shape((devices, 128), F32),
        ),
        [
            pltpu.VMEM((tokens + 8, channels), F32),
            pltpu.VMEM((tokens + 8, channels), F32),
            pltpu.VMEM((8, channels + 2 * 128), F32),
        ],
    )(carry, act, slope, bx, ady, grads, inputs, rim, raw, flags, power, conv_weight, step_bias, skip)

    terms = lax.all_to_all(terms, ("dp",) + CTX, 0, 0, tiled=True)
    width = channels // devices
    shard = jnp.sum(terms, axis=0)[: (KERNEL + 1) * width].reshape(KERNEL + 1, width)
    shard = shard * (1.0 / (dp_size * length))
    back = shifted(head[: KERNEL - 1], CTX, -1)
    edge = jnp.concatenate([edge[: 16 - (KERNEL - 1)], edge[16 - (KERNEL - 1) :] + back], 0)
    grad_input = lax.dynamic_update_slice(out, edge.astype(BF16), (tokens - 16, 0))
    return (grad_input[None], grad_raw[None], shard[:KERNEL][:, None, :], shard[KERNEL][None, :])


def solution(mesh):
    sizes = mesh.shape
    shape = (sizes["dp"], sizes["ctx"] // SPLIT, SPLIT, sizes["tp"])
    mesh = jax.sharding.Mesh(mesh.devices.reshape(shape), ("dp",) + CTX + ("tp",))
    return jax.shard_map(
        body,
        mesh=mesh,
        in_specs=(
            P("dp", CTX, "tp"),
            P("dp", CTX, "tp"),
            P("dp", CTX),
            P("tp"),
            P(None, "tp"),
            P("tp"),
            P("tp"),
            P("tp"),
            P("dp", CTX, "tp"),
        ),
        out_specs=(
            P("dp", CTX, "tp"),
            P("dp", CTX, "tp"),
            P(None, "tp", ("dp",) + CTX),
            P("tp", ("dp",) + CTX),
        ),
        check_vma=False,
    )
```

```python
import math

import jax
import jax.numpy as jnp
from jax import lax
from jax.experimental import pallas as pl
from jax.experimental.pallas import tpu as pltpu
from jax.sharding import PartitionSpec as P

BLOCK = 128
HEAD_WIDTH = 64
STATE = 128
KERNEL = 4
SPLIT = 4
ROWS = STATE // SPLIT
EXTRA = 128
WIDE = 60 * 1024 * 1024
NARROW = 16 * 1024 * 1024
F32 = jnp.float32
BF16 = jnp.bfloat16
CTX = ("ch", "cl")


def mm(left, right):
    return jnp.dot(left, right, preferred_element_type=F32)


def mm_nt(left, right):
    return lax.dot_general(left, right, (((1,), (1,)), ((), ())), preferred_element_type=F32)


def mm_tn(left, right):
    return lax.dot_general(left, right, (((0,), (0,)), ((), ())), preferred_element_type=F32)


def pieces_of(value, count):
    out = []
    for _ in range(count):
        piece = value.astype(BF16)
        out.append(piece)
        value = value - piece.astype(F32)
    return out


def exact_left(ones, value, count):
    return sum(mm(ones, piece) for piece in pieces_of(value, count))


def exact_right(value, ones, count):
    return sum(mm(piece, ones) for piece in pieces_of(value, count))


def spread_matrix(rows, columns):
    row = lax.broadcasted_iota(jnp.int32, (rows, columns), 0)
    lane = lax.broadcasted_iota(jnp.int32, (rows, columns), 1)
    return jnp.where((lane >> 6) == row, 1.0, 0.0).astype(BF16)


def gather_matrix(rows, columns):
    row = lax.broadcasted_iota(jnp.int32, (rows, columns), 0)
    lane = lax.broadcasted_iota(jnp.int32, (rows, columns), 1)
    return jnp.where((row >> 6) == lane, 1.0, 0.0).astype(BF16)


def spread_heads(value, spread, count):
    return sum(mm_tn(piece, spread) for piece in pieces_of(value, count))


def column(line):
    heads = line.shape[1]
    row = lax.broadcasted_iota(jnp.int32, (heads, heads), 0)
    lane = lax.broadcasted_iota(jnp.int32, (heads, heads), 1)
    return jnp.sum(jnp.where(row == lane, line, jnp.zeros_like(line)), axis=1, keepdims=True)


def softplus(value):
    small = jnp.exp(-jnp.abs(value))
    series = small * (1.0 - small * (0.5 - small * (1.0 / 3.0 - small * 0.25)))
    return jnp.maximum(value, 0.0) + jnp.where(small < 0.01, series, jnp.log(1.0 + small))


def triangles():
    row = lax.broadcasted_iota(jnp.int32, (BLOCK, BLOCK), 0)
    lane = lax.broadcasted_iota(jnp.int32, (BLOCK, BLOCK), 1)
    return jnp.where(row >= lane, 1.0, 0.0), jnp.where(row <= lane, 1.0, 0.0)


def block_marks(flags):
    lower, upper = triangles()
    seg_col = jnp.sum(lower * flags, axis=1, keepdims=True)
    seg_row = mm(jnp.broadcast_to(flags, (8, BLOCK)).astype(BF16), upper.astype(BF16))[0:1]
    last = jnp.sum(flags, axis=1, keepdims=True)
    mask = jnp.where(seg_col == seg_row, lower, 0.0)
    alive = jnp.where(seg_col == 0.0, 1.0, 0.0)
    tail = jnp.where(seg_col == last, 1.0, 0.0)
    alive_last = jnp.where(last == 0.0, 1.0, 0.0)
    return mask, alive, tail, alive_last


def head_steps(raw, bias, power, length):
    rate = -0.5 * jnp.exp((power.astype(F32) / 3.0 - 1.0) * math.log(length))
    return softplus(raw + column(bias)), column(rate)


def block_scales(step, rate):
    upper = triangles()[1].astype(BF16)
    cum = exact_right(step * rate, upper, 3)
    total = cum[:, BLOCK - 1 : BLOCK]
    middle = 0.5 * total
    return jnp.exp(cum - middle), step * jnp.exp(middle - cum), jnp.exp(middle), jnp.exp(total)


def wide_lines(half, through, spread):
    lane = lax.broadcasted_iota(jnp.int32, (half.shape[0], 8), 1)
    lines = spread_heads(jnp.where(lane == 0, half, through), spread, 3)
    return lines[0:1], lines[1:2]


def silu_rows(padded, weight, bias_ref, start, cols):
    total = jnp.broadcast_to(bias_ref[:, cols], (64, 128))
    for tap in range(KERNEL):
        at = 8 - (KERNEL - 1) + start + tap
        total = total + padded[at : at + 64, cols] * weight[tap : tap + 1, cols]
    return total, 1.0 / (1.0 + jnp.exp(-total))


def fill_padded(padded, rim, inputs):
    tokens, channels = inputs.shape
    padded[0:8, :] = jnp.zeros((8, channels), F32)
    padded[8 - (KERNEL - 1) : 8, :] = rim.astype(F32)
    padded[8 : 8 + tokens, :] = inputs.astype(F32)


def front_kernel(
    length, input_hbm, rim_hbm, grad_hbm, raw_hbm, flags_hbm, power_hbm, step_bias_hbm, weight_hbm, bias_hbm,
    act_hbm, bx_hbm, ady_hbm, pack_hbm,
    input_ref, rim_ref, grad_ref, raw_ref, flags_ref, power_ref, step_bias_ref, weight_ref, bias_ref,
    act_ref, bx_ref, ady_ref, pack_ref, padded, sems,
):
    pairs = (
        (raw_hbm, raw_ref),
        (step_bias_hbm, step_bias_ref),
        (power_hbm, power_ref),
        (flags_hbm, flags_ref),
        (input_hbm, input_ref),
        (rim_hbm, rim_ref),
        (weight_hbm, weight_ref),
        (bias_hbm, bias_ref),
        (grad_hbm, grad_ref),
        (act_ref, act_hbm),
        (bx_ref, bx_hbm),
        (ady_ref, ady_hbm),
        (pack_ref, pack_hbm),
    )
    copies = [pltpu.make_async_copy(source, target, sems.at[i]) for i, (source, target) in enumerate(pairs)]
    for copy in copies[:9]:
        copy.start()
    tokens, channels = input_ref.shape
    heads = raw_ref.shape[0]
    inner = heads * HEAD_WIDTH
    blocks = tokens // BLOCK
    spread = spread_matrix(heads, inner)
    for copy in copies[:4]:
        copy.wait()
    step, rate = head_steps(raw_ref[...], step_bias_ref[...], power_ref[...], length)
    flags = flags_ref[...].astype(F32)
    marks = [block_marks(flags[block : block + 1]) for block in range(blocks)]
    scales = [block_scales(step[:, block * BLOCK : (block + 1) * BLOCK], rate) for block in range(blocks)]
    for copy in copies[4:8]:
        copy.wait()
    fill_padded(padded, rim_ref[...], input_ref[...])
    weight = weight_ref[...].astype(F32)
    for low in range(0, channels, 128):
        cols = slice(low, low + 128)
        for start in range(0, tokens, 64):
            total, gate = silu_rows(padded, weight, bias_ref, start, cols)
            act_ref[start : start + 64, cols] = (total * gate).astype(BF16)
    copies[9].start()
    copies[8].wait()
    fresh, back, passing = [], [], []
    passing_heads = jnp.ones((heads, 1), F32)
    for block in range(blocks):
        rows = slice(block * BLOCK, (block + 1) * BLOCK)
        _, alive, tail, alive_last = marks[block]
        row_scale, col_scale, half, whole = scales[block]
        through = whole * alive_last
        passing_heads = passing_heads * through
        half_wide, through_wide = wide_lines(half, through, spread)
        bx = (act_ref[rows, 0:inner].astype(F32) * spread_heads(col_scale, spread, 2)).astype(BF16)
        ady = (grad_ref[rows, :].astype(F32) * spread_heads(row_scale, spread, 2)).astype(BF16)
        bx_ref[rows, :] = bx
        ady_ref[rows, :] = ady
        keys = (act_ref[rows, inner : inner + STATE].astype(F32) * tail).astype(BF16)
        queries = (act_ref[rows, inner + STATE : inner + 2 * STATE].astype(F32) * alive).astype(BF16)
        fresh.append(mm_tn(keys, bx) * half_wide)
        back.append(mm_tn(queries, ady) * half_wide)
        passing.append(through_wide)
    copies[10].start()
    copies[11].start()
    up = fresh[0]
    for block in range(1, blocks):
        up = passing[block] * up + fresh[block]
    down = back[blocks - 1]
    for block in range(blocks - 2, -1, -1):
        down = passing[block] * down + back[block]
    pack_ref[:, :, 0:inner] = jnp.concatenate(
        [up.reshape(SPLIT, ROWS, inner), down.reshape(SPLIT, ROWS, inner)], axis=1
    ).astype(BF16)
    row = lax.broadcasted_iota(jnp.int32, (heads, EXTRA), 0)
    lane = lax.broadcasted_iota(jnp.int32, (heads, EXTRA), 1)
    wide = jnp.sum(jnp.where(row == lane, passing_heads, 0.0), axis=0, keepdims=True)
    pack_ref[:, :, inner : inner + EXTRA] = jnp.broadcast_to(
        stacked(wide, 2 * ROWS)[None], (SPLIT, 2 * ROWS, EXTRA)
    )
    copies[12].start()
    for copy in copies[9:]:
        copy.wait()


def stacked(value, rows):
    hi, mid, lo = [piece.astype(F32) for piece in pieces_of(value, 3)]
    line = lax.broadcasted_iota(jnp.int32, (rows, EXTRA), 0)
    return jnp.where(line == 0, hi, jnp.where(line == 1, mid, jnp.where(line == 2, lo, 0.0))).astype(BF16)


def passed(pack_ref, source, inner, spread):
    lines = pack_ref[source, 0:16, inner : inner + EXTRA]
    return (
        jnp.sum(lines.astype(F32), axis=0, keepdims=True),
        jnp.sum(mm(lines, spread), axis=0, keepdims=True),
    )


def totals_kernel(near_ref, out_ref):
    inner = near_ref.shape[2] - EXTRA
    group = lax.axis_index("ch")
    spread = spread_matrix(EXTRA, inner)
    decay = [passed(near_ref, source, inner, spread) for source in range(SPLIT)]
    up = jnp.zeros((ROWS, inner), F32)
    down = jnp.zeros((ROWS, inner), F32)
    through = jnp.ones((1, EXTRA), F32)
    for source in range(SPLIT):
        up = decay[source][1] * up + near_ref[source, 0:ROWS, 0:inner].astype(F32)
        through = through * decay[source][0]
    for source in range(SPLIT - 1, -1, -1):
        down = decay[source][1] * down + near_ref[source, ROWS : 2 * ROWS, 0:inner].astype(F32)
    lines = stacked(through, ROWS)
    for target in range(SPLIT):
        later = jnp.where(target > group, 1.0, 0.0)
        out_ref[target, :, 0:inner] = (later * up + (1.0 - later) * down).astype(BF16)
        out_ref[target, :, inner : inner + EXTRA] = lines


def states_kernel(near_ref, far_ref, out_ref):
    inner = near_ref.shape[2] - EXTRA
    group = lax.axis_index("ch")
    spread = spread_matrix(EXTRA, inner)
    near = [passed(near_ref, source, inner, spread)[1] for source in range(SPLIT)]
    far = [passed(far_ref, source, inner, spread)[1] for source in range(SPLIT)]
    up = jnp.zeros((ROWS, inner), F32)
    down = jnp.zeros((ROWS, inner), F32)
    for source in range(SPLIT):
        use = jnp.where(source < group, 1.0, 0.0)
        up = (use * far[source] + (1.0 - use)) * up + use * far_ref[source, :, 0:inner].astype(F32)
    for source in range(SPLIT - 1, -1, -1):
        use = jnp.where(source > group, 1.0, 0.0)
        down = (use * far[source] + (1.0 - use)) * down + use * far_ref[source, :, 0:inner].astype(F32)
    for source in range(SPLIT):
        out_ref[source, 0:ROWS, :] = up.astype(BF16)
        up = near[source] * up + near_ref[source, 0:ROWS, 0:inner].astype(F32)
    for source in range(SPLIT - 1, -1, -1):
        out_ref[source, ROWS : 2 * ROWS, :] = down.astype(BF16)
        down = near[source] * down + near_ref[source, ROWS : 2 * ROWS, 0:inner].astype(F32)


def local_kernel(
    length, input_ref, rim_ref, grad_ref, raw_ref, flags_ref, power_ref, step_bias_ref, skip_ref, weight_ref, bias_ref,
    act_ref, bx_ref, ady_ref,
    dpre_ref, reach_ref, sums_ref, heads_ref, marked_ref, inside_ref, lines_ref, meets_ref, sides_ref, base_ref,
    padded, slope_ref, product,
):
    tokens, channels = act_ref.shape
    inner = bx_ref.shape[1]
    heads = inner // HEAD_WIDTH
    blocks = tokens // BLOCK
    fill_padded(padded, rim_ref[...], input_ref[...])
    weight = weight_ref[...].astype(F32)
    for low in range(0, channels, 128):
        cols = slice(low, low + 128)
        for start in range(0, tokens, 64):
            total, gate = silu_rows(padded, weight, bias_ref, start, cols)
            slope_ref[start : start + 64, cols] = gate * (1.0 + total * (1.0 - gate))
    step, rate = head_steps(raw_ref[...], step_bias_ref[...], power_ref[...], length)
    heads_ref[0:heads, :] = step
    heads_ref[heads : 2 * heads, :] = 1.0 / (1.0 + jnp.exp(-(raw_ref[...] + column(step_bias_ref[...]))))
    heads_ref[2 * heads : 3 * heads, :] = jnp.broadcast_to(rate, (heads, tokens))
    spread = spread_matrix(heads, inner)
    gather = gather_matrix(inner, heads)
    flags = flags_ref[...].astype(F32)
    skip_wide = spread_heads(jnp.broadcast_to(column(skip_ref[...]), (heads, 8)), spread, 3)[0:1]
    key_cols, query_cols = slice(inner, inner + STATE), slice(inner + STATE, channels)
    for block in range(blocks):
        rows = slice(block * BLOCK, (block + 1) * BLOCK)
        mask, alive, tail, alive_last = block_marks(flags[block : block + 1])
        _, col_scale, half, whole = block_scales(step[:, rows], rate)
        half_wide, through_wide = wide_lines(half, whole * alive_last, spread)
        lines_ref[2 * block : 2 * block + 1, :] = half_wide
        lines_ref[2 * block + 1 : 2 * block + 2, :] = through_wide
        bx = bx_ref[rows, :]
        ady = ady_ref[rows, :]
        key = act_ref[rows, key_cols]
        query = act_ref[rows, query_cols]
        keys = (key.astype(F32) * tail).astype(BF16)
        queries = (query.astype(F32) * alive).astype(BF16)
        marked_ref[rows, 0:STATE] = keys
        marked_ref[rows, STATE : 2 * STATE] = queries
        if block < blocks - 1:
            inside_ref[block] = mm_tn(keys, bx) * half_wide
        if block > 0:
            inside_ref[blocks - 2 + block] = mm_tn(queries, ady) * half_wide
        scores = mask * mm_nt(query, key)
        scores_t = scores.T.astype(BF16)
        dbx = mm(scores_t, ady)
        col_sum = exact_right(bx.astype(F32) * dbx, gather, 2)
        row_sum = exact_right(ady.astype(F32) * mm(scores.astype(BF16), bx), gather, 2)
        sums_ref[0:heads, rows] = (row_sum - col_sum).T
        sums_ref[heads : 2 * heads, rows] = col_sum.T
        dscores = mask * mm_nt(ady, bx)
        dscores_t = dscores.T.astype(BF16)
        dquery = mm(dscores.astype(BF16), key)
        dkey = mm(dscores_t, query)
        slope = slope_ref[rows, 0:inner]
        reach = slope * spread_heads(col_scale, spread, 2)
        reach_ref[rows, 0:inner] = reach
        reach_ref[rows, key_cols] = slope_ref[rows, key_cols] * tail
        reach_ref[rows, query_cols] = slope_ref[rows, query_cols] * alive
        dpre_ref[rows, 0:inner] = reach * dbx + slope * (skip_wide * grad_ref[rows, :].astype(F32))
        dpre_ref[rows, key_cols] = dkey * slope_ref[rows, key_cols]
        dpre_ref[rows, query_cols] = dquery * slope_ref[rows, query_cols]
    lines_ref[2 * blocks :, :] = jnp.zeros((lines_ref.shape[0] - 2 * blocks, inner), F32)
    line = lax.broadcasted_iota(jnp.int32, (8, 128), 0)
    for low in range(0, channels, 128):
        cols = slice(low, low + 128)
        found = jnp.zeros((8, 128), F32)
        for tap in range(KERNEL + 1):
            acc = jnp.zeros((8, 128), F32)
            for start in range(0, tokens, 64):
                rows = slice(start, start + 64)
                at = 8 - (KERNEL - 1) + start + tap
                here, meets = dpre_ref[rows, cols], reach_ref[rows, cols]
                if tap < KERNEL:
                    other = padded[at : at + 64, cols]
                    here, meets = here * other, meets * other
                acc = acc + jnp.sum(here.reshape(8, 8, 128), axis=0)
                if low < inner:
                    product[tap, rows, cols] = meets.astype(BF16)
                else:
                    sides_ref[tap, rows, low - inner : low - inner + 128] = meets.astype(BF16)
            found = jnp.where(line == tap, jnp.sum(acc, axis=0, keepdims=True), found)
        base_ref[:, cols] = found
    line = lax.broadcasted_iota(jnp.int32, (8, inner), 0)
    found = base_ref[:, 0:inner]
    for tap in range(KERNEL + 1):
        through = jnp.ones((1, inner), F32)
        own = jnp.zeros((STATE, inner), F32)
        total = jnp.zeros((STATE, inner), F32)
        for block in range(blocks - 1, -1, -1):
            rows = slice(block * BLOCK, (block + 1) * BLOCK)
            meets = mm_tn(marked_ref[rows, 0:STATE], product[tap, rows, :]) * lines_ref[2 * block : 2 * block + 1, :]
            total = total + through * meets
            if block < blocks - 1:
                found = found + jnp.where(line == tap, jnp.sum(own * meets, axis=0, keepdims=True), 0.0)
            if block > 0:
                decay = lines_ref[2 * block + 1 : 2 * block + 2, :]
                through = decay * through
                own = decay * own + inside_ref[blocks - 2 + block]
        meets_ref[tap] = total.astype(BF16)
    base_ref[:, 0:inner] = found


def block_states(carry_ref, inside_ref, lines_ref, blocks):
    inner = carry_ref.shape[2]
    entering = carry_ref[:, 0:ROWS, :].astype(F32).reshape(STATE, inner)
    leaving = carry_ref[:, ROWS : 2 * ROWS, :].astype(F32).reshape(STATE, inner)
    states, grads = [entering], [leaving]
    for block in range(blocks - 1):
        through = lines_ref[2 * block + 1 : 2 * block + 2, :]
        states.append(through * states[-1] + inside_ref[block])
    for block in range(blocks - 1, 0, -1):
        through = lines_ref[2 * block + 1 : 2 * block + 2, :]
        grads.append(through * grads[-1] + inside_ref[blocks - 2 + block])
    return states, grads[::-1]


def taps_kernel(
    carry_hbm, lines_hbm, inside_hbm, bx_hbm, ady_hbm, marked_hbm, part_hbm, reach_hbm, weight_hbm, meets_hbm, sides_hbm,
    base_hbm,
    head_ref, terms_ref,
    carry_ref, lines_ref, inside_ref, bx_ref, ady_ref, marked_ref, part_ref, reach_ref, weight_ref, meets_ref,
    sides_ref, base_ref, sums_ref, sems,
):
    top = part_ref.shape[0]
    pairs = (
        (carry_hbm, carry_ref),
        (lines_hbm, lines_ref),
        (inside_hbm, inside_ref),
        (bx_hbm, bx_ref),
        (ady_hbm, ady_ref),
        (marked_hbm.at[0:top], marked_ref),
        (part_hbm.at[0:top], part_ref),
        (reach_hbm.at[0:top], reach_ref),
        (weight_hbm, weight_ref),
        (sides_hbm, sides_ref),
        (base_hbm, base_ref),
        (meets_hbm, meets_ref),
    )
    copies = [pltpu.make_async_copy(source, target, sems.at[i]) for i, (source, target) in enumerate(pairs)]
    for copy in copies:
        copy.start()
    channels = part_ref.shape[1]
    tokens, inner = bx_ref.shape
    blocks = tokens // BLOCK
    line = lax.broadcasted_iota(jnp.int32, (8, 128), 0)
    for copy in copies[:9]:
        copy.wait()
    states, grads = block_states(carry_ref, inside_ref, lines_ref, blocks)
    keys, queries = [], []
    for block in range(blocks):
        rows = slice(block * BLOCK, (block + 1) * BLOCK)
        half = lines_ref[2 * block : 2 * block + 1, :]
        grad = (half * grads[block]).astype(BF16)
        keys.append(mm_nt(bx_ref[rows, :], grad))
        queries.append(mm_nt(ady_ref[rows, :], (half * states[block]).astype(BF16)))
        if block == 0:
            first = part_ref[:, 0:inner] + reach_ref[:, 0:inner] * mm(marked_ref[:, 0:STATE], grad)
    key_cols, query_cols = slice(inner, inner + STATE), slice(inner + STATE, channels)
    first = [
        first[0:8],
        (part_ref[:, key_cols] + reach_ref[:, key_cols] * keys[0][0:top])[0:8],
        (part_ref[:, query_cols] + reach_ref[:, query_cols] * queries[0][0:top])[0:8],
    ]
    weight = weight_ref[...].astype(F32)
    for part, cols in zip(first, (slice(0, inner), key_cols, query_cols)):
        wide = lax.broadcasted_iota(jnp.int32, part.shape, 0)
        lines = jnp.zeros(part.shape, F32)
        for at in range(KERNEL - 1):
            row = sum(weight[tap : tap + 1, cols] * part[at - tap : at - tap + 1] for tap in range(at + 1))
            lines = jnp.where(wide == at, row, lines)
        head_ref[:, cols] = lines
    for copy in copies[9:11]:
        copy.wait()
    for side, parts in enumerate((keys, queries)):
        cols = slice(side * STATE, (side + 1) * STATE)
        out = slice(inner + side * STATE, inner + (side + 1) * STATE)
        found = base_ref[:, out]
        for tap in range(KERNEL + 1):
            acc = jnp.zeros((8, STATE), F32)
            for block in range(blocks):
                rows = slice(block * BLOCK, (block + 1) * BLOCK)
                met = parts[block] * sides_ref[tap, rows, cols].astype(F32)
                acc = acc + jnp.sum(met.reshape(BLOCK // 8, 8, STATE), axis=0)
            found = found + jnp.where(line == tap, jnp.sum(acc, axis=0, keepdims=True), 0.0)
        sums_ref[:, out] = found
    copies[11].wait()
    for low in range(0, inner, 128):
        cols = slice(low, low + 128)
        grad = carry_ref[:, ROWS : 2 * ROWS, cols].astype(F32).reshape(STATE, 128)
        found = base_ref[:, cols]
        for tap in range(KERNEL + 1):
            met = grad * meets_ref[tap, :, cols].astype(F32)
            acc = jnp.sum(met.reshape(STATE // 8, 8, 128), axis=0)
            found = found + jnp.where(line == tap, jnp.sum(acc, axis=0, keepdims=True), 0.0)
        sums_ref[:, cols] = found

    targets = terms_ref.shape[0]
    width = channels // targets
    lane = lax.broadcasted_iota(jnp.int32, (8, 128), 1)
    own = (lane >= line * width) & (lane < (line + 1) * width) & (line <= KERNEL)
    for tile in range(channels // 128, sums_ref.shape[1] // 128):
        sums_ref[:, tile * 128 : tile * 128 + 128] = jnp.zeros((8, 128), F32)
    aside = pltpu.roll(sums_ref[...], 0, 1, stride=width // 2, stride_axis=0)
    sums_ref[...] = pltpu.roll(aside, 0, 1, stride=width - width // 2, stride_axis=0)
    for target in range(targets):
        tile, at = divmod(target * width, 128)
        part = sums_ref[:, tile * 128 : tile * 128 + 128]
        if at:
            part = jnp.where(lane >= at, part, sums_ref[:, tile * 128 + 128 : tile * 128 + 256])
            part = pltpu.roll(part, 128 - at, 1)
        terms_ref[target : target + 1, :] = jnp.sum(jnp.where(own, part, 0.0), axis=0, keepdims=True)


def rest_kernel(
    carry_ref, marked_ref, bx_ref, ady_ref, part_ref, reach_ref, inside_ref, lines_ref, sums_ref, heads_ref, weight_ref,
    back_ref,
    out_ref, raw_out_ref, dpre, after,
):
    tokens, channels = part_ref.shape
    inner = bx_ref.shape[1]
    heads = inner // HEAD_WIDTH
    blocks = tokens // BLOCK
    key_cols, query_cols = slice(inner, inner + STATE), slice(inner + STATE, channels)
    gather = gather_matrix(inner, heads)
    lower = triangles()[0].astype(BF16)
    at_last = jnp.where(lax.broadcasted_iota(jnp.int32, (heads, BLOCK), 1) == BLOCK - 1, 1.0, 0.0)
    states, grads = block_states(carry_ref, inside_ref, lines_ref, blocks)
    for block in range(blocks):
        rows = slice(block * BLOCK, (block + 1) * BLOCK)
        half = lines_ref[2 * block : 2 * block + 1, :]
        through = lines_ref[2 * block + 1 : 2 * block + 2, :]
        state = (half * states[block]).astype(BF16)
        grad = (half * grads[block]).astype(BF16)
        keys = marked_ref[rows, 0:STATE]
        queries = marked_ref[rows, STATE : 2 * STATE]
        bx = bx_ref[rows, :]
        ady = ady_ref[rows, :]
        dbx = mm(keys, grad)
        dpre[rows, 0:inner] = part_ref[rows, 0:inner] + reach_ref[rows, 0:inner] * dbx
        dpre[rows, key_cols] = part_ref[rows, key_cols] + reach_ref[rows, key_cols] * mm_nt(bx, grad)
        dpre[rows, query_cols] = part_ref[rows, query_cols] + reach_ref[rows, query_cols] * mm_nt(ady, state)
        row_sum = exact_right(ady.astype(F32) * mm(queries, state), gather, 2)
        col_sum = exact_right(bx.astype(F32) * dbx, gather, 2)
        whole = jnp.sum(
            grad.astype(F32) * mm_tn(keys, bx) + through * (grads[block] * states[block]), axis=0, keepdims=True
        )
        whole = exact_right(jnp.broadcast_to(whole, (8, inner)), gather, 3)
        dcum = sums_ref[0:heads, rows] + (row_sum - col_sum).T + at_last * column(whole[0:1])
        dlog = exact_right(dcum, lower, 3)
        step, gate, rate = (heads_ref[i * heads : (i + 1) * heads, rows] for i in range(3))
        raw_out_ref[:, rows] = ((sums_ref[heads : 2 * heads, rows] + col_sum.T) / step + rate * dlog) * gate
    dpre[tokens : tokens + 8, :] = jnp.zeros((8, channels), F32)
    after[...] = jnp.zeros((8, channels), F32)
    after[8 - (KERNEL - 1) : 8, :] = back_ref[...]
    weight = weight_ref[...].astype(F32)
    for low in range(0, channels, 128):
        cols = slice(low, low + 128)
        for start in range(0, tokens, 64):
            total = dpre[start : start + 64, cols] * weight[KERNEL - 1 : KERNEL, cols]
            for tap in range(KERNEL - 1):
                ahead = start + KERNEL - 1 - tap
                total = total + dpre[ahead : ahead + 64, cols] * weight[tap : tap + 1, cols]
            if start == tokens - 64:
                total = jnp.concatenate([total[0:56], total[56:64] + after[:, cols]], axis=0)
            out_ref[start : start + 64, cols] = total.astype(BF16)


def shares_kernel(scale, terms_ref, weight_ref, bias_ref):
    total = jnp.sum(terms_ref[...], axis=0) * scale
    width = bias_ref.shape[1]
    for tap in range(KERNEL):
        weight_ref[tap, :, :] = total[:, tap * width : (tap + 1) * width]
    bias_ref[...] = total[:, KERNEL * width : (KERNEL + 1) * width]


def call(kernel, out_shape, scratch=(), flops=0, moved=0, vmem=WIDE, **specs):
    return pl.pallas_call(
        kernel,
        out_shape=out_shape,
        scratch_shapes=list(scratch),
        compiler_params=pltpu.CompilerParams(vmem_limit_bytes=vmem),
        cost_estimate=pl.CostEstimate(flops=flops, bytes_accessed=moved, transcendentals=0),
        **specs,
    )


def shifted(value, axis, by):
    devices = lax.axis_size(axis)
    pairs = [(i, i + by) for i in range(devices) if 0 <= i + by < devices]
    return lax.ppermute(value, axis, pairs)


def body(
    conv_input, step_raw, doc_starts, decay_power, conv_weight, conv_bias, step_bias, skip_gain, grad_out
):
    tokens, channels = conv_input.shape[1:]
    heads = step_raw.shape[2]
    inner = heads * HEAD_WIDTH
    ctx_size = lax.axis_size(CTX)
    dp_size = lax.axis_size("dp")
    devices = dp_size * ctx_size
    length = tokens * ctx_size
    inputs = conv_input[0]
    rim = shifted(inputs[tokens - (KERNEL - 1) :], CTX, 1)
    blocks = tokens // BLOCK
    shape = jax.ShapeDtypeStruct
    padded = pltpu.VMEM((tokens + 8, channels), F32)
    placed = pl.BlockSpec(memory_space=pltpu.HBM)
    held = pl.BlockSpec(memory_space=pltpu.VMEM)
    grads = grad_out[0]
    raw = step_raw[0].T
    flags = doc_starts.reshape(blocks, BLOCK)
    power, step_bias, skip, bias = decay_power[None], step_bias[None], skip_gain[None], conv_bias[None]

    def buffers(*arrays):
        return [pltpu.VMEM(array.shape, array.dtype) for array in arrays]

    sources = (inputs, rim, grads, raw, flags, power, step_bias, conv_weight, bias)
    results = (
        shape((tokens, channels), BF16),
        shape((tokens, inner), BF16),
        shape((tokens, inner), BF16),
        shape((SPLIT, 2 * ROWS, inner + EXTRA), BF16),
    )
    act, bx, ady, pack = call(
        lambda *refs: front_kernel(length, *refs),
        results,
        buffers(*sources, *results) + [padded, pltpu.SemaphoreType.DMA((len(sources) + len(results),))],
        in_specs=[placed] * len(sources),
        out_specs=(placed,) * len(results),
    )(*sources)

    part, reach, sums, per_head, marked, inside, lines, meets, sides, base = call(
        lambda *refs: local_kernel(length, *refs),
        (
            shape((tokens, channels), F32),
            shape((tokens, channels), F32),
            shape((2 * heads, tokens), F32),
            shape((3 * heads, tokens), F32),
            shape((tokens, 2 * STATE), BF16),
            shape((2 * (blocks - 1), STATE, inner), F32),
            shape((8, inner), F32),
            shape((KERNEL + 1, STATE, inner), BF16),
            shape((KERNEL + 1, tokens, 2 * STATE), BF16),
            shape((8, channels), F32),
        ),
        [padded, pltpu.VMEM((tokens, channels), F32), pltpu.VMEM((KERNEL + 1, tokens, inner), BF16)],
        flops=10**9,
        moved=10**7,
    )(inputs, rim, grads, raw, flags, power, step_bias, skip, conv_weight, bias, act, bx, ady)

    near = lax.all_to_all(pack, "cl", 0, 0, tiled=True)
    totals = call(totals_kernel, shape((SPLIT, ROWS, inner + EXTRA), BF16), vmem=NARROW)(near)
    far = lax.all_to_all(totals, "ch", 0, 0, tiled=True)
    far, lines = lax.optimization_barrier((far, lines))
    states = call(
        states_kernel,
        shape((SPLIT, 2 * ROWS, inner), BF16),
        vmem=NARROW,
    )(near, far)
    carry = lax.all_to_all(states, "cl", 0, 0, tiled=True)

    sources = (carry, lines, inside, bx, ady, marked, part, reach, conv_weight, meets, sides, base)
    tops = [shape((16,) + a.shape[1:], a.dtype) if a is marked or a is part or a is reach else a for a in sources]
    head, terms = call(
        taps_kernel,
        (shape((8, channels), F32), shape((devices, 128), F32)),
        buffers(*tops) + [pltpu.VMEM((8, channels + 2 * 128), F32), pltpu.SemaphoreType.DMA((len(sources),))],
        in_specs=[placed] * len(sources),
    )(*sources)

    terms = lax.all_to_all(terms.reshape(devices, 1, 128), ("dp",) + CTX, 0, 0, tiled=True)
    back = shifted(head[: KERNEL - 1], CTX, -1)
    out, grad_raw = call(
        rest_kernel,
        (shape((tokens, channels), BF16), shape((heads, tokens), F32)),
        [padded, pltpu.VMEM((8, channels), F32)],
        flops=10**9,
        moved=10**7,
    )(carry, marked, bx, ady, part, reach, inside, lines, sums, per_head, conv_weight, back)
    width = channels // devices
    grad_weight, grad_bias = call(
        lambda *refs: shares_kernel(1.0 / (dp_size * length), *refs),
        (shape((KERNEL, 1, width), F32), shape((1, width), F32)),
        vmem=NARROW,
    )(terms)
    return (out[None], grad_raw.T[None], grad_weight, grad_bias)


def solution(mesh):
    sizes = mesh.shape
    shape = (sizes["dp"], sizes["ctx"] // SPLIT, SPLIT, sizes["tp"])
    mesh = jax.sharding.Mesh(mesh.devices.reshape(shape), ("dp",) + CTX + ("tp",))
    return jax.shard_map(
        body,
        mesh=mesh,
        in_specs=(
            P("dp", CTX, "tp"),
            P("dp", CTX, "tp"),
            P("dp", CTX),
            P("tp"),
            P(None, "tp"),
            P("tp"),
            P("tp"),
            P("tp"),
            P("dp", CTX, "tp"),
        ),
        out_specs=(
            P("dp", CTX, "tp"),
            P("dp", CTX, "tp"),
            P(None, "tp", ("dp",) + CTX),
            P("tp", ("dp",) + CTX),
        ),
        check_vma=False,
    )
```

```python
import math

import jax
import jax.numpy as jnp
from jax import lax
from jax.experimental import pallas as pl
from jax.experimental.pallas import tpu as pltpu
from jax.sharding import PartitionSpec as P

BLOCK = 128
HEAD_WIDTH = 64
STATE = 128
KERNEL = 4
SPLIT = 4
ROWS = STATE // SPLIT
EXTRA = 128
WIDE = 60 * 1024 * 1024
NARROW = 16 * 1024 * 1024
F32 = jnp.float32
BF16 = jnp.bfloat16
CTX = ("ch", "cl")
NEAR = (2, 1, 0, 3)


def mm(left, right):
    return jnp.dot(left, right, preferred_element_type=F32)


def mm_nt(left, right):
    return lax.dot_general(left, right, (((1,), (1,)), ((), ())), preferred_element_type=F32)


def mm_tn(left, right):
    return lax.dot_general(left, right, (((0,), (0,)), ((), ())), preferred_element_type=F32)


def pieces_of(value, count):
    out = []
    for _ in range(count):
        piece = value.astype(BF16)
        out.append(piece)
        value = value - piece.astype(F32)
    return out


def exact_left(ones, value, count):
    return sum(mm(ones, piece) for piece in pieces_of(value, count))


def exact_right(value, ones, count):
    return sum(mm(piece, ones) for piece in pieces_of(value, count))


def spread_matrix(rows, columns):
    row = lax.broadcasted_iota(jnp.int32, (rows, columns), 0)
    lane = lax.broadcasted_iota(jnp.int32, (rows, columns), 1)
    return jnp.where((lane >> 6) == row, 1.0, 0.0).astype(BF16)


def gather_matrix(rows, columns):
    row = lax.broadcasted_iota(jnp.int32, (rows, columns), 0)
    lane = lax.broadcasted_iota(jnp.int32, (rows, columns), 1)
    return jnp.where((row >> 6) == lane, 1.0, 0.0).astype(BF16)


def spread_heads(value, spread, count):
    return sum(mm_tn(piece, spread) for piece in pieces_of(value, count))


def column(line):
    heads = line.shape[1]
    row = lax.broadcasted_iota(jnp.int32, (heads, heads), 0)
    lane = lax.broadcasted_iota(jnp.int32, (heads, heads), 1)
    return jnp.sum(jnp.where(row == lane, line, jnp.zeros_like(line)), axis=1, keepdims=True)


def softplus(value):
    small = jnp.exp(-jnp.abs(value))
    series = small * (1.0 - small * (0.5 - small * (1.0 / 3.0 - small * 0.25)))
    return jnp.maximum(value, 0.0) + jnp.where(small < 0.01, series, jnp.log(1.0 + small))


def triangles():
    row = lax.broadcasted_iota(jnp.int32, (BLOCK, BLOCK), 0)
    lane = lax.broadcasted_iota(jnp.int32, (BLOCK, BLOCK), 1)
    return jnp.where(row >= lane, 1.0, 0.0), jnp.where(row <= lane, 1.0, 0.0)


def block_marks(flags):
    lower, upper = triangles()
    seg_col = jnp.sum(lower * flags, axis=1, keepdims=True)
    seg_row = mm(jnp.broadcast_to(flags, (8, BLOCK)).astype(BF16), upper.astype(BF16))[0:1]
    last = jnp.sum(flags, axis=1, keepdims=True)
    mask = jnp.where(seg_col == seg_row, lower, 0.0)
    alive = jnp.where(seg_col == 0.0, 1.0, 0.0)
    tail = jnp.where(seg_col == last, 1.0, 0.0)
    alive_last = jnp.where(last == 0.0, 1.0, 0.0)
    return mask, alive, tail, alive_last


def head_steps(raw, bias, power, length):
    rate = -0.5 * jnp.exp((power.astype(F32) / 3.0 - 1.0) * math.log(length))
    return softplus(raw + column(bias)), column(rate)


def block_scales(step, rate):
    upper = triangles()[1].astype(BF16)
    cum = exact_right(step * rate, upper, 3)
    total = cum[:, BLOCK - 1 : BLOCK]
    middle = 0.5 * total
    return jnp.exp(cum - middle), step * jnp.exp(middle - cum), jnp.exp(middle), jnp.exp(total)


def wide_lines(half, through, spread):
    lane = lax.broadcasted_iota(jnp.int32, (half.shape[0], 8), 1)
    lines = spread_heads(jnp.where(lane == 0, half, through), spread, 3)
    return lines[0:1], lines[1:2]


def silu_rows(padded, weight, bias_ref, start, cols):
    total = jnp.broadcast_to(bias_ref[:, cols], (64, 128))
    for tap in range(KERNEL):
        at = 8 - (KERNEL - 1) + start + tap
        total = total + padded[at : at + 64, cols] * weight[tap : tap + 1, cols]
    return total, 1.0 / (1.0 + jnp.exp(-total))


def fill_padded(padded, rim, inputs):
    tokens, channels = inputs.shape
    padded[0:8, :] = jnp.zeros((8, channels), F32)
    padded[8 - (KERNEL - 1) : 8, :] = rim.astype(F32)
    padded[8 : 8 + tokens, :] = inputs.astype(F32)


def front_kernel(
    length, input_hbm, rim_hbm, grad_hbm, raw_hbm, flags_hbm, power_hbm, step_bias_hbm, weight_hbm, bias_hbm,
    act_hbm, bx_hbm, ady_hbm, pack_hbm,
    input_ref, rim_ref, grad_ref, raw_ref, flags_ref, power_ref, step_bias_ref, weight_ref, bias_ref,
    act_ref, bx_ref, ady_ref, pack_ref, padded, sems,
):
    pairs = (
        (raw_hbm, raw_ref),
        (step_bias_hbm, step_bias_ref),
        (power_hbm, power_ref),
        (flags_hbm, flags_ref),
        (input_hbm, input_ref),
        (rim_hbm, rim_ref),
        (weight_hbm, weight_ref),
        (bias_hbm, bias_ref),
        (grad_hbm, grad_ref),
        (act_ref, act_hbm),
        (bx_ref, bx_hbm),
        (ady_ref, ady_hbm),
        (pack_ref, pack_hbm),
    )
    copies = [pltpu.make_async_copy(source, target, sems.at[i]) for i, (source, target) in enumerate(pairs)]
    for copy in copies[:9]:
        copy.start()
    tokens, channels = input_ref.shape
    heads = raw_ref.shape[0]
    inner = heads * HEAD_WIDTH
    blocks = tokens // BLOCK
    spread = spread_matrix(heads, inner)
    for copy in copies[:4]:
        copy.wait()
    step, rate = head_steps(raw_ref[...], step_bias_ref[...], power_ref[...], length)
    flags = flags_ref[...].astype(F32)
    marks = [block_marks(flags[block : block + 1]) for block in range(blocks)]
    scales = [block_scales(step[:, block * BLOCK : (block + 1) * BLOCK], rate) for block in range(blocks)]
    for copy in copies[4:8]:
        copy.wait()
    fill_padded(padded, rim_ref[...], input_ref[...])
    weight = weight_ref[...].astype(F32)
    for low in range(0, channels, 128):
        cols = slice(low, low + 128)
        for start in range(0, tokens, 64):
            total, gate = silu_rows(padded, weight, bias_ref, start, cols)
            act_ref[start : start + 64, cols] = (total * gate).astype(BF16)
    copies[9].start()
    copies[8].wait()
    fresh, back, passing = [], [], []
    passing_heads = jnp.ones((heads, 1), F32)
    for block in range(blocks):
        rows = slice(block * BLOCK, (block + 1) * BLOCK)
        _, alive, tail, alive_last = marks[block]
        row_scale, col_scale, half, whole = scales[block]
        through = whole * alive_last
        passing_heads = passing_heads * through
        half_wide, through_wide = wide_lines(half, through, spread)
        bx = (act_ref[rows, 0:inner].astype(F32) * spread_heads(col_scale, spread, 2)).astype(BF16)
        ady = (grad_ref[rows, :].astype(F32) * spread_heads(row_scale, spread, 2)).astype(BF16)
        bx_ref[rows, :] = bx
        ady_ref[rows, :] = ady
        keys = (act_ref[rows, inner : inner + STATE].astype(F32) * tail).astype(BF16)
        queries = (act_ref[rows, inner + STATE : inner + 2 * STATE].astype(F32) * alive).astype(BF16)
        fresh.append(mm_tn(keys, bx) * half_wide)
        back.append(mm_tn(queries, ady) * half_wide)
        passing.append(through_wide)
    copies[10].start()
    copies[11].start()
    up = fresh[0]
    for block in range(1, blocks):
        up = passing[block] * up + fresh[block]
    down = back[blocks - 1]
    for block in range(blocks - 2, -1, -1):
        down = passing[block] * down + back[block]
    for place, source in enumerate(NEAR):
        rows = slice(source * ROWS, (source + 1) * ROWS)
        pack_ref[place, :, 0:inner] = jnp.concatenate([up[rows], down[rows]], axis=0).astype(BF16)
    row = lax.broadcasted_iota(jnp.int32, (heads, EXTRA), 0)
    lane = lax.broadcasted_iota(jnp.int32, (heads, EXTRA), 1)
    wide = jnp.sum(jnp.where(row == lane, passing_heads, 0.0), axis=0, keepdims=True)
    pack_ref[:, :, inner : inner + EXTRA] = jnp.broadcast_to(
        stacked(wide, 2 * ROWS)[None], (SPLIT, 2 * ROWS, EXTRA)
    )
    copies[12].start()
    for copy in copies[9:]:
        copy.wait()


def stacked(value, rows):
    hi, mid, lo = [piece.astype(F32) for piece in pieces_of(value, 3)]
    line = lax.broadcasted_iota(jnp.int32, (rows, EXTRA), 0)
    return jnp.where(line == 0, hi, jnp.where(line == 1, mid, jnp.where(line == 2, lo, 0.0))).astype(BF16)


def passed(pack_ref, source, inner, spread):
    lines = pack_ref[source, 0:16, inner : inner + EXTRA]
    return (
        jnp.sum(lines.astype(F32), axis=0, keepdims=True),
        jnp.sum(mm(lines, spread), axis=0, keepdims=True),
    )


def near_place(place):
    return NEAR.index(place)


def far_place(group):
    return (group + SPLIT // 2) % SPLIT


def totals_kernel(near_ref, out_ref):
    inner = near_ref.shape[2] - EXTRA
    group = lax.axis_index("ch")
    spread = spread_matrix(EXTRA, inner)
    decay = [passed(near_ref, near_place(source), inner, spread) for source in range(SPLIT)]
    up = jnp.zeros((ROWS, inner), F32)
    down = jnp.zeros((ROWS, inner), F32)
    through = jnp.ones((1, EXTRA), F32)
    for source in range(SPLIT):
        up = decay[source][1] * up + near_ref[near_place(source), 0:ROWS, 0:inner].astype(F32)
        through = through * decay[source][0]
    for source in range(SPLIT - 1, -1, -1):
        down = decay[source][1] * down + near_ref[near_place(source), ROWS : 2 * ROWS, 0:inner].astype(F32)
    lines = stacked(through, ROWS)
    for target in range(SPLIT):
        later = jnp.where(target > group, 1.0, 0.0)
        out_ref[far_place(target), :, 0:inner] = (later * up + (1.0 - later) * down).astype(BF16)
        out_ref[far_place(target), :, inner : inner + EXTRA] = lines


def states_kernel(near_ref, far_ref, out_ref):
    inner = near_ref.shape[2] - EXTRA
    group = lax.axis_index("ch")
    spread = spread_matrix(EXTRA, inner)
    near = [passed(near_ref, near_place(source), inner, spread)[1] for source in range(SPLIT)]
    far = [passed(far_ref, far_place(source), inner, spread)[1] for source in range(SPLIT)]
    up = jnp.zeros((ROWS, inner), F32)
    down = jnp.zeros((ROWS, inner), F32)
    for source in range(SPLIT):
        use = jnp.where(source < group, 1.0, 0.0)
        up = (use * far[source] + (1.0 - use)) * up + use * far_ref[far_place(source), :, 0:inner].astype(F32)
    for source in range(SPLIT - 1, -1, -1):
        use = jnp.where(source > group, 1.0, 0.0)
        down = (use * far[source] + (1.0 - use)) * down + use * far_ref[far_place(source), :, 0:inner].astype(F32)
    for source in range(SPLIT):
        out_ref[near_place(source), 0:ROWS, :] = up.astype(BF16)
        up = near[source] * up + near_ref[near_place(source), 0:ROWS, 0:inner].astype(F32)
    for source in range(SPLIT - 1, -1, -1):
        out_ref[near_place(source), ROWS : 2 * ROWS, :] = down.astype(BF16)
        down = near[source] * down + near_ref[near_place(source), ROWS : 2 * ROWS, 0:inner].astype(F32)


def local_kernel(
    length, input_ref, rim_ref, grad_ref, raw_ref, flags_ref, power_ref, step_bias_ref, skip_ref, weight_ref, bias_ref,
    act_ref, bx_ref, ady_ref,
    dpre_ref, reach_ref, sums_ref, heads_ref, marked_ref, inside_ref, lines_ref, meets_ref, sides_ref, base_ref,
    padded, slope_ref, product,
):
    tokens, channels = act_ref.shape
    inner = bx_ref.shape[1]
    heads = inner // HEAD_WIDTH
    blocks = tokens // BLOCK
    fill_padded(padded, rim_ref[...], input_ref[...])
    weight = weight_ref[...].astype(F32)
    for low in range(0, channels, 128):
        cols = slice(low, low + 128)
        for start in range(0, tokens, 64):
            total, gate = silu_rows(padded, weight, bias_ref, start, cols)
            slope_ref[start : start + 64, cols] = gate * (1.0 + total * (1.0 - gate))
    step, rate = head_steps(raw_ref[...], step_bias_ref[...], power_ref[...], length)
    heads_ref[0:heads, :] = step
    heads_ref[heads : 2 * heads, :] = 1.0 / (1.0 + jnp.exp(-(raw_ref[...] + column(step_bias_ref[...]))))
    heads_ref[2 * heads : 3 * heads, :] = jnp.broadcast_to(rate, (heads, tokens))
    spread = spread_matrix(heads, inner)
    gather = gather_matrix(inner, heads)
    flags = flags_ref[...].astype(F32)
    skip_wide = spread_heads(jnp.broadcast_to(column(skip_ref[...]), (heads, 8)), spread, 3)[0:1]
    key_cols, query_cols = slice(inner, inner + STATE), slice(inner + STATE, channels)
    for block in range(blocks):
        rows = slice(block * BLOCK, (block + 1) * BLOCK)
        mask, alive, tail, alive_last = block_marks(flags[block : block + 1])
        _, col_scale, half, whole = block_scales(step[:, rows], rate)
        half_wide, through_wide = wide_lines(half, whole * alive_last, spread)
        lines_ref[2 * block : 2 * block + 1, :] = half_wide
        lines_ref[2 * block + 1 : 2 * block + 2, :] = through_wide
        bx = bx_ref[rows, :]
        ady = ady_ref[rows, :]
        key = act_ref[rows, key_cols]
        query = act_ref[rows, query_cols]
        keys = (key.astype(F32) * tail).astype(BF16)
        queries = (query.astype(F32) * alive).astype(BF16)
        marked_ref[rows, 0:STATE] = keys
        marked_ref[rows, STATE : 2 * STATE] = queries
        if block < blocks - 1:
            inside_ref[block] = mm_tn(keys, bx) * half_wide
        if block > 0:
            inside_ref[blocks - 2 + block] = mm_tn(queries, ady) * half_wide
        scores = mask * mm_nt(query, key)
        scores_t = scores.T.astype(BF16)
        dbx = mm(scores_t, ady)
        col_sum = exact_right(bx.astype(F32) * dbx, gather, 2)
        row_sum = exact_right(ady.astype(F32) * mm(scores.astype(BF16), bx), gather, 2)
        sums_ref[0:heads, rows] = (row_sum - col_sum).T
        sums_ref[heads : 2 * heads, rows] = col_sum.T
        dscores = mask * mm_nt(ady, bx)
        dscores_t = dscores.T.astype(BF16)
        dquery = mm(dscores.astype(BF16), key)
        dkey = mm(dscores_t, query)
        slope = slope_ref[rows, 0:inner]
        reach = slope * spread_heads(col_scale, spread, 2)
        reach_ref[rows, 0:inner] = reach
        reach_ref[rows, key_cols] = slope_ref[rows, key_cols] * tail
        reach_ref[rows, query_cols] = slope_ref[rows, query_cols] * alive
        dpre_ref[rows, 0:inner] = reach * dbx + slope * (skip_wide * grad_ref[rows, :].astype(F32))
        dpre_ref[rows, key_cols] = dkey * slope_ref[rows, key_cols]
        dpre_ref[rows, query_cols] = dquery * slope_ref[rows, query_cols]
    lines_ref[2 * blocks :, :] = jnp.zeros((lines_ref.shape[0] - 2 * blocks, inner), F32)
    line = lax.broadcasted_iota(jnp.int32, (8, 128), 0)
    for low in range(0, channels, 128):
        cols = slice(low, low + 128)
        found = jnp.zeros((8, 128), F32)
        for tap in range(KERNEL + 1):
            acc = jnp.zeros((8, 128), F32)
            for start in range(0, tokens, 64):
                rows = slice(start, start + 64)
                at = 8 - (KERNEL - 1) + start + tap
                here, meets = dpre_ref[rows, cols], reach_ref[rows, cols]
                if tap < KERNEL:
                    other = padded[at : at + 64, cols]
                    here, meets = here * other, meets * other
                acc = acc + jnp.sum(here.reshape(8, 8, 128), axis=0)
                if low < inner:
                    product[tap, rows, cols] = meets.astype(BF16)
                else:
                    sides_ref[tap, rows, low - inner : low - inner + 128] = meets.astype(BF16)
            found = jnp.where(line == tap, jnp.sum(acc, axis=0, keepdims=True), found)
        base_ref[:, cols] = found
    line = lax.broadcasted_iota(jnp.int32, (8, inner), 0)
    found = base_ref[:, 0:inner]
    for tap in range(KERNEL + 1):
        through = jnp.ones((1, inner), F32)
        own = jnp.zeros((STATE, inner), F32)
        total = jnp.zeros((STATE, inner), F32)
        for block in range(blocks - 1, -1, -1):
            rows = slice(block * BLOCK, (block + 1) * BLOCK)
            meets = mm_tn(marked_ref[rows, 0:STATE], product[tap, rows, :]) * lines_ref[2 * block : 2 * block + 1, :]
            total = total + through * meets
            if block < blocks - 1:
                found = found + jnp.where(line == tap, jnp.sum(own * meets, axis=0, keepdims=True), 0.0)
            if block > 0:
                decay = lines_ref[2 * block + 1 : 2 * block + 2, :]
                through = decay * through
                own = decay * own + inside_ref[blocks - 2 + block]
        meets_ref[tap] = total.astype(BF16)
    base_ref[:, 0:inner] = found


def block_states(carry_ref, inside_ref, lines_ref, blocks):
    entering, leaving = (
        jnp.concatenate([carry_ref[near_place(i), low : low + ROWS, :].astype(F32) for i in range(SPLIT)], axis=0)
        for low in (0, ROWS)
    )
    states, grads = [entering], [leaving]
    for block in range(blocks - 1):
        through = lines_ref[2 * block + 1 : 2 * block + 2, :]
        states.append(through * states[-1] + inside_ref[block])
    for block in range(blocks - 1, 0, -1):
        through = lines_ref[2 * block + 1 : 2 * block + 2, :]
        grads.append(through * grads[-1] + inside_ref[blocks - 2 + block])
    return states, grads[::-1]


def taps_kernel(
    carry_hbm, lines_hbm, inside_hbm, bx_hbm, ady_hbm, marked_hbm, part_hbm, reach_hbm, weight_hbm, meets_hbm, sides_hbm,
    base_hbm,
    head_ref, terms_ref,
    carry_ref, lines_ref, inside_ref, bx_ref, ady_ref, marked_ref, part_ref, reach_ref, weight_ref, meets_ref,
    sides_ref, base_ref, sums_ref, sems,
):
    top = part_ref.shape[0]
    pairs = (
        (carry_hbm, carry_ref),
        (lines_hbm, lines_ref),
        (inside_hbm, inside_ref),
        (bx_hbm, bx_ref),
        (ady_hbm, ady_ref),
        (marked_hbm.at[0:top], marked_ref),
        (part_hbm.at[0:top], part_ref),
        (reach_hbm.at[0:top], reach_ref),
        (weight_hbm, weight_ref),
        (sides_hbm, sides_ref),
        (base_hbm, base_ref),
        (meets_hbm, meets_ref),
    )
    copies = [pltpu.make_async_copy(source, target, sems.at[i]) for i, (source, target) in enumerate(pairs)]
    for copy in copies:
        copy.start()
    channels = part_ref.shape[1]
    tokens, inner = bx_ref.shape
    blocks = tokens // BLOCK
    line = lax.broadcasted_iota(jnp.int32, (8, 128), 0)
    for copy in copies[:9]:
        copy.wait()
    states, grads = block_states(carry_ref, inside_ref, lines_ref, blocks)
    keys, queries = [], []
    for block in range(blocks):
        rows = slice(block * BLOCK, (block + 1) * BLOCK)
        half = lines_ref[2 * block : 2 * block + 1, :]
        grad = (half * grads[block]).astype(BF16)
        keys.append(mm_nt(bx_ref[rows, :], grad))
        queries.append(mm_nt(ady_ref[rows, :], (half * states[block]).astype(BF16)))
        if block == 0:
            first = part_ref[:, 0:inner] + reach_ref[:, 0:inner] * mm(marked_ref[:, 0:STATE], grad)
    key_cols, query_cols = slice(inner, inner + STATE), slice(inner + STATE, channels)
    first = [
        first[0:8],
        (part_ref[:, key_cols] + reach_ref[:, key_cols] * keys[0][0:top])[0:8],
        (part_ref[:, query_cols] + reach_ref[:, query_cols] * queries[0][0:top])[0:8],
    ]
    weight = weight_ref[...].astype(F32)
    for part, cols in zip(first, (slice(0, inner), key_cols, query_cols)):
        wide = lax.broadcasted_iota(jnp.int32, part.shape, 0)
        lines = jnp.zeros(part.shape, F32)
        for at in range(KERNEL - 1):
            row = sum(weight[tap : tap + 1, cols] * part[at - tap : at - tap + 1] for tap in range(at + 1))
            lines = jnp.where(wide == at, row, lines)
        head_ref[:, cols] = lines
    for copy in copies[9:11]:
        copy.wait()
    for side, parts in enumerate((keys, queries)):
        cols = slice(side * STATE, (side + 1) * STATE)
        out = slice(inner + side * STATE, inner + (side + 1) * STATE)
        found = base_ref[:, out]
        for tap in range(KERNEL + 1):
            acc = jnp.zeros((8, STATE), F32)
            for block in range(blocks):
                rows = slice(block * BLOCK, (block + 1) * BLOCK)
                met = parts[block] * sides_ref[tap, rows, cols].astype(F32)
                acc = acc + jnp.sum(met.reshape(BLOCK // 8, 8, STATE), axis=0)
            found = found + jnp.where(line == tap, jnp.sum(acc, axis=0, keepdims=True), 0.0)
        sums_ref[:, out] = found
    copies[11].wait()
    for low in range(0, inner, 128):
        cols = slice(low, low + 128)
        grad = jnp.concatenate(
            [carry_ref[near_place(i), ROWS : 2 * ROWS, cols].astype(F32) for i in range(SPLIT)], axis=0
        )
        found = base_ref[:, cols]
        for tap in range(KERNEL + 1):
            met = grad * meets_ref[tap, :, cols].astype(F32)
            acc = jnp.sum(met.reshape(STATE // 8, 8, 128), axis=0)
            found = found + jnp.where(line == tap, jnp.sum(acc, axis=0, keepdims=True), 0.0)
        sums_ref[:, cols] = found

    targets = terms_ref.shape[0]
    width = channels // targets
    lane = lax.broadcasted_iota(jnp.int32, (8, 128), 1)
    own = (lane >= line * width) & (lane < (line + 1) * width) & (line <= KERNEL)
    for tile in range(channels // 128, sums_ref.shape[1] // 128):
        sums_ref[:, tile * 128 : tile * 128 + 128] = jnp.zeros((8, 128), F32)
    aside = pltpu.roll(sums_ref[...], 0, 1, stride=width // 2, stride_axis=0)
    sums_ref[...] = pltpu.roll(aside, 0, 1, stride=width - width // 2, stride_axis=0)
    for target in range(targets):
        tile, at = divmod(target * width, 128)
        part = sums_ref[:, tile * 128 : tile * 128 + 128]
        if at:
            part = jnp.where(lane >= at, part, sums_ref[:, tile * 128 + 128 : tile * 128 + 256])
            part = pltpu.roll(part, 128 - at, 1)
        terms_ref[target : target + 1, :] = jnp.sum(jnp.where(own, part, 0.0), axis=0, keepdims=True)


def rest_kernel(
    carry_ref, marked_ref, bx_ref, ady_ref, part_ref, reach_ref, inside_ref, lines_ref, sums_ref, heads_ref, weight_ref,
    back_ref,
    out_ref, raw_out_ref, dpre, after,
):
    tokens, channels = part_ref.shape
    inner = bx_ref.shape[1]
    heads = inner // HEAD_WIDTH
    blocks = tokens // BLOCK
    key_cols, query_cols = slice(inner, inner + STATE), slice(inner + STATE, channels)
    gather = gather_matrix(inner, heads)
    lower = triangles()[0].astype(BF16)
    at_last = jnp.where(lax.broadcasted_iota(jnp.int32, (heads, BLOCK), 1) == BLOCK - 1, 1.0, 0.0)
    states, grads = block_states(carry_ref, inside_ref, lines_ref, blocks)
    for block in range(blocks):
        rows = slice(block * BLOCK, (block + 1) * BLOCK)
        half = lines_ref[2 * block : 2 * block + 1, :]
        through = lines_ref[2 * block + 1 : 2 * block + 2, :]
        state = (half * states[block]).astype(BF16)
        grad = (half * grads[block]).astype(BF16)
        keys = marked_ref[rows, 0:STATE]
        queries = marked_ref[rows, STATE : 2 * STATE]
        bx = bx_ref[rows, :]
        ady = ady_ref[rows, :]
        dbx = mm(keys, grad)
        dpre[rows, 0:inner] = part_ref[rows, 0:inner] + reach_ref[rows, 0:inner] * dbx
        dpre[rows, key_cols] = part_ref[rows, key_cols] + reach_ref[rows, key_cols] * mm_nt(bx, grad)
        dpre[rows, query_cols] = part_ref[rows, query_cols] + reach_ref[rows, query_cols] * mm_nt(ady, state)
        row_sum = exact_right(ady.astype(F32) * mm(queries, state), gather, 2)
        col_sum = exact_right(bx.astype(F32) * dbx, gather, 2)
        whole = jnp.sum(
            grad.astype(F32) * mm_tn(keys, bx) + through * (grads[block] * states[block]), axis=0, keepdims=True
        )
        whole = exact_right(jnp.broadcast_to(whole, (8, inner)), gather, 3)
        dcum = sums_ref[0:heads, rows] + (row_sum - col_sum).T + at_last * column(whole[0:1])
        dlog = exact_right(dcum, lower, 3)
        step, gate, rate = (heads_ref[i * heads : (i + 1) * heads, rows] for i in range(3))
        raw_out_ref[:, rows] = ((sums_ref[heads : 2 * heads, rows] + col_sum.T) / step + rate * dlog) * gate
    dpre[tokens : tokens + 8, :] = jnp.zeros((8, channels), F32)
    after[...] = jnp.zeros((8, channels), F32)
    after[8 - (KERNEL - 1) : 8, :] = back_ref[...]
    weight = weight_ref[...].astype(F32)
    for low in range(0, channels, 128):
        cols = slice(low, low + 128)
        for start in range(0, tokens, 64):
            total = dpre[start : start + 64, cols] * weight[KERNEL - 1 : KERNEL, cols]
            for tap in range(KERNEL - 1):
                ahead = start + KERNEL - 1 - tap
                total = total + dpre[ahead : ahead + 64, cols] * weight[tap : tap + 1, cols]
            if start == tokens - 64:
                total = jnp.concatenate([total[0:56], total[56:64] + after[:, cols]], axis=0)
            out_ref[start : start + 64, cols] = total.astype(BF16)


def shares_kernel(scale, terms_ref, weight_ref, bias_ref):
    total = jnp.sum(terms_ref[...], axis=0) * scale
    width = bias_ref.shape[1]
    for tap in range(KERNEL):
        weight_ref[tap, :, :] = total[:, tap * width : (tap + 1) * width]
    bias_ref[...] = total[:, KERNEL * width : (KERNEL + 1) * width]


def call(kernel, out_shape, scratch=(), flops=0, moved=0, vmem=WIDE, **specs):
    return pl.pallas_call(
        kernel,
        out_shape=out_shape,
        scratch_shapes=list(scratch),
        compiler_params=pltpu.CompilerParams(vmem_limit_bytes=vmem),
        cost_estimate=pl.CostEstimate(flops=flops, bytes_accessed=moved, transcendentals=0),
        **specs,
    )


def shifted(value, axis, by):
    devices = lax.axis_size(axis)
    pairs = [(i, i + by) for i in range(devices) if 0 <= i + by < devices]
    return lax.ppermute(value, axis, pairs)


def body(
    conv_input, step_raw, doc_starts, decay_power, conv_weight, conv_bias, step_bias, skip_gain, grad_out
):
    tokens, channels = conv_input.shape[1:]
    heads = step_raw.shape[2]
    inner = heads * HEAD_WIDTH
    ctx_size = lax.axis_size(CTX)
    dp_size = lax.axis_size("dp")
    devices = dp_size * ctx_size
    length = tokens * ctx_size
    inputs = conv_input[0]
    rim = shifted(inputs[tokens - (KERNEL - 1) :], CTX, 1)
    blocks = tokens // BLOCK
    shape = jax.ShapeDtypeStruct
    padded = pltpu.VMEM((tokens + 8, channels), F32)
    placed = pl.BlockSpec(memory_space=pltpu.HBM)
    held = pl.BlockSpec(memory_space=pltpu.VMEM)
    grads = grad_out[0]
    raw = step_raw[0].T
    flags = doc_starts.reshape(blocks, BLOCK)
    power, step_bias, skip, bias = decay_power[None], step_bias[None], skip_gain[None], conv_bias[None]

    def buffers(*arrays):
        return [pltpu.VMEM(array.shape, array.dtype) for array in arrays]

    sources = (inputs, rim, grads, raw, flags, power, step_bias, conv_weight, bias)
    results = (
        shape((tokens, channels), BF16),
        shape((tokens, inner), BF16),
        shape((tokens, inner), BF16),
        shape((SPLIT, 2 * ROWS, inner + EXTRA), BF16),
    )
    act, bx, ady, pack = call(
        lambda *refs: front_kernel(length, *refs),
        results,
        buffers(*sources, *results) + [padded, pltpu.SemaphoreType.DMA((len(sources) + len(results),))],
        in_specs=[placed] * len(sources),
        out_specs=(placed,) * len(results),
    )(*sources)

    part, reach, sums, per_head, marked, inside, lines, meets, sides, base = call(
        lambda *refs: local_kernel(length, *refs),
        (
            shape((tokens, channels), F32),
            shape((tokens, channels), F32),
            shape((2 * heads, tokens), F32),
            shape((3 * heads, tokens), F32),
            shape((tokens, 2 * STATE), BF16),
            shape((2 * (blocks - 1), STATE, inner), F32),
            shape((8, inner), F32),
            shape((KERNEL + 1, STATE, inner), BF16),
            shape((KERNEL + 1, tokens, 2 * STATE), BF16),
            shape((8, channels), F32),
        ),
        [padded, pltpu.VMEM((tokens, channels), F32), pltpu.VMEM((KERNEL + 1, tokens, inner), BF16)],
        flops=10**9,
        moved=10**7,
    )(inputs, rim, grads, raw, flags, power, step_bias, skip, conv_weight, bias, act, bx, ady)

    near = lax.all_to_all(pack, "cl", 0, 0, tiled=True, axis_index_groups=[list(NEAR)])
    totals = call(totals_kernel, shape((SPLIT, ROWS, inner + EXTRA), BF16), vmem=NARROW)(near)
    turned = [[far_place(place) for place in range(SPLIT)]]
    far = lax.all_to_all(totals, "ch", 0, 0, tiled=True, axis_index_groups=turned)
    far, lines = lax.optimization_barrier((far, lines))
    states = call(
        states_kernel,
        shape((SPLIT, 2 * ROWS, inner), BF16),
        vmem=NARROW,
    )(near, far)
    carry = lax.all_to_all(states, "cl", 0, 0, tiled=True, axis_index_groups=[list(NEAR)])

    sources = (carry, lines, inside, bx, ady, marked, part, reach, conv_weight, meets, sides, base)
    tops = [shape((16,) + a.shape[1:], a.dtype) if a is marked or a is part or a is reach else a for a in sources]
    head, terms = call(
        taps_kernel,
        (shape((8, channels), F32), shape((devices, 128), F32)),
        buffers(*tops) + [pltpu.VMEM((8, channels + 2 * 128), F32), pltpu.SemaphoreType.DMA((len(sources),))],
        in_specs=[placed] * len(sources),
    )(*sources)

    terms = lax.all_to_all(terms.reshape(devices, 1, 128), ("dp",) + CTX, 0, 0, tiled=True)
    back = shifted(head[: KERNEL - 1], CTX, -1)
    out, grad_raw = call(
        rest_kernel,
        (shape((tokens, channels), BF16), shape((heads, tokens), F32)),
        [padded, pltpu.VMEM((8, channels), F32)],
        flops=10**9,
        moved=10**7,
    )(carry, marked, bx, ady, part, reach, inside, lines, sums, per_head, conv_weight, back)
    width = channels // devices
    grad_weight, grad_bias = call(
        lambda *refs: shares_kernel(1.0 / (dp_size * length), *refs),
        (shape((KERNEL, 1, width), F32), shape((1, width), F32)),
        vmem=NARROW,
    )(terms)
    return (out[None], grad_raw.T[None], grad_weight, grad_bias)


def solution(mesh):
    sizes = mesh.shape
    shape = (sizes["dp"], sizes["ctx"] // SPLIT, SPLIT, sizes["tp"])
    mesh = jax.sharding.Mesh(mesh.devices.reshape(shape), ("dp",) + CTX + ("tp",))
    return jax.shard_map(
        body,
        mesh=mesh,
        in_specs=(
            P("dp", CTX, "tp"),
            P("dp", CTX, "tp"),
            P("dp", CTX),
            P("tp"),
            P(None, "tp"),
            P("tp"),
            P("tp"),
            P("tp"),
            P("dp", CTX, "tp"),
        ),
        out_specs=(
            P("dp", CTX, "tp"),
            P("dp", CTX, "tp"),
            P(None, "tp", ("dp",) + CTX),
            P("tp", ("dp",) + CTX),
        ),
        check_vma=False,
    )
```

```python
import math

import jax
import jax.numpy as jnp
from jax import lax
from jax.experimental import pallas as pl
from jax.experimental.pallas import tpu as pltpu
from jax.sharding import PartitionSpec as P

BLOCK = 128
HEAD_WIDTH = 64
STATE = 128
KERNEL = 4
SPLIT = 4
ROWS = STATE // SPLIT
EXTRA = 128
WIDE = 60 * 1024 * 1024
NARROW = 16 * 1024 * 1024
F32 = jnp.float32
BF16 = jnp.bfloat16
CTX = ("ch", "cl")
NEAR = (2, 1, 0, 3)


def mm(left, right):
    return jnp.dot(left, right, preferred_element_type=F32)


def mm_nt(left, right):
    return lax.dot_general(left, right, (((1,), (1,)), ((), ())), preferred_element_type=F32)


def mm_tn(left, right):
    return lax.dot_general(left, right, (((0,), (0,)), ((), ())), preferred_element_type=F32)


def pieces_of(value, count):
    out = []
    for _ in range(count):
        piece = value.astype(BF16)
        out.append(piece)
        value = value - piece.astype(F32)
    return out


def exact_left(ones, value, count):
    return sum(mm(ones, piece) for piece in pieces_of(value, count))


def exact_right(value, ones, count):
    return sum(mm(piece, ones) for piece in pieces_of(value, count))


def spread_matrix(rows, columns):
    row = lax.broadcasted_iota(jnp.int32, (rows, columns), 0)
    lane = lax.broadcasted_iota(jnp.int32, (rows, columns), 1)
    return jnp.where((lane >> 6) == row, 1.0, 0.0).astype(BF16)


def gather_matrix(rows, columns):
    row = lax.broadcasted_iota(jnp.int32, (rows, columns), 0)
    lane = lax.broadcasted_iota(jnp.int32, (rows, columns), 1)
    return jnp.where((row >> 6) == lane, 1.0, 0.0).astype(BF16)


def spread_heads(value, spread, count):
    return sum(mm_tn(piece, spread) for piece in pieces_of(value, count))


def column(line):
    heads = line.shape[1]
    row = lax.broadcasted_iota(jnp.int32, (heads, heads), 0)
    lane = lax.broadcasted_iota(jnp.int32, (heads, heads), 1)
    return jnp.sum(jnp.where(row == lane, line, jnp.zeros_like(line)), axis=1, keepdims=True)


def softplus(value):
    small = jnp.exp(-jnp.abs(value))
    series = small * (1.0 - small * (0.5 - small * (1.0 / 3.0 - small * 0.25)))
    return jnp.maximum(value, 0.0) + jnp.where(small < 0.01, series, jnp.log(1.0 + small))


def triangles():
    row = lax.broadcasted_iota(jnp.int32, (BLOCK, BLOCK), 0)
    lane = lax.broadcasted_iota(jnp.int32, (BLOCK, BLOCK), 1)
    return jnp.where(row >= lane, 1.0, 0.0), jnp.where(row <= lane, 1.0, 0.0)


def block_marks(flags):
    lower, upper = triangles()
    seg_col = jnp.sum(lower * flags, axis=1, keepdims=True)
    seg_row = mm(jnp.broadcast_to(flags, (8, BLOCK)).astype(BF16), upper.astype(BF16))[0:1]
    last = jnp.sum(flags, axis=1, keepdims=True)
    mask = jnp.where(seg_col == seg_row, lower, 0.0)
    alive = jnp.where(seg_col == 0.0, 1.0, 0.0)
    tail = jnp.where(seg_col == last, 1.0, 0.0)
    alive_last = jnp.where(last == 0.0, 1.0, 0.0)
    return mask, alive, tail, alive_last


def head_steps(raw, bias, power, length):
    rate = -0.5 * jnp.exp((power.astype(F32) / 3.0 - 1.0) * math.log(length))
    return softplus(raw + column(bias)), column(rate)


def block_scales(step, rate):
    upper = triangles()[1].astype(BF16)
    cum = exact_right(step * rate, upper, 3)
    total = cum[:, BLOCK - 1 : BLOCK]
    middle = 0.5 * total
    return jnp.exp(cum - middle), step * jnp.exp(middle - cum), jnp.exp(middle), jnp.exp(total)


def wide_lines(half, through, spread):
    lane = lax.broadcasted_iota(jnp.int32, (half.shape[0], 8), 1)
    lines = spread_heads(jnp.where(lane == 0, half, through), spread, 3)
    return lines[0:1], lines[1:2]


def silu_rows(padded, weight, bias_ref, start, cols):
    total = jnp.broadcast_to(bias_ref[:, cols], (64, 128))
    for tap in range(KERNEL):
        at = 8 - (KERNEL - 1) + start + tap
        total = total + padded[at : at + 64, cols] * weight[tap : tap + 1, cols]
    return total, 1.0 / (1.0 + jnp.exp(-total))


def fill_padded(padded, rim, inputs):
    tokens, channels = inputs.shape
    padded[0:8, :] = jnp.zeros((8, channels), F32)
    padded[8 - (KERNEL - 1) : 8, :] = rim.astype(F32)
    padded[8 : 8 + tokens, :] = inputs.astype(F32)


def front_kernel(
    length, input_hbm, rim_hbm, grad_hbm, raw_hbm, flags_hbm, power_hbm, step_bias_hbm, weight_hbm, bias_hbm,
    act_hbm, bx_hbm, ady_hbm, pack_hbm,
    input_ref, rim_ref, grad_ref, raw_ref, flags_ref, power_ref, step_bias_ref, weight_ref, bias_ref,
    act_ref, bx_ref, ady_ref, pack_ref, padded, sems,
):
    pairs = (
        (raw_hbm, raw_ref),
        (step_bias_hbm, step_bias_ref),
        (power_hbm, power_ref),
        (flags_hbm, flags_ref),
        (input_hbm, input_ref),
        (rim_hbm, rim_ref),
        (weight_hbm, weight_ref),
        (bias_hbm, bias_ref),
        (grad_hbm, grad_ref),
        (act_ref, act_hbm),
        (bx_ref, bx_hbm),
        (ady_ref, ady_hbm),
        (pack_ref, pack_hbm),
    )
    copies = [pltpu.make_async_copy(source, target, sems.at[i]) for i, (source, target) in enumerate(pairs)]
    for copy in copies[:9]:
        copy.start()
    tokens, channels = input_ref.shape
    heads = raw_ref.shape[0]
    inner = heads * HEAD_WIDTH
    blocks = tokens // BLOCK
    spread = spread_matrix(heads, inner)
    for copy in copies[:4]:
        copy.wait()
    step, rate = head_steps(raw_ref[...], step_bias_ref[...], power_ref[...], length)
    flags = flags_ref[...].astype(F32)
    marks = [block_marks(flags[block : block + 1]) for block in range(blocks)]
    scales = [block_scales(step[:, block * BLOCK : (block + 1) * BLOCK], rate) for block in range(blocks)]
    for copy in copies[4:8]:
        copy.wait()
    fill_padded(padded, rim_ref[...], input_ref[...])
    weight = weight_ref[...].astype(F32)
    for low in range(0, channels, 128):
        cols = slice(low, low + 128)
        for start in range(0, tokens, 64):
            total, gate = silu_rows(padded, weight, bias_ref, start, cols)
            act_ref[start : start + 64, cols] = (total * gate).astype(BF16)
    copies[9].start()
    copies[8].wait()
    fresh, back, passing = [], [], []
    passing_heads = jnp.ones((heads, 1), F32)
    for block in range(blocks):
        rows = slice(block * BLOCK, (block + 1) * BLOCK)
        _, alive, tail, alive_last = marks[block]
        row_scale, col_scale, half, whole = scales[block]
        through = whole * alive_last
        passing_heads = passing_heads * through
        half_wide, through_wide = wide_lines(half, through, spread)
        bx = (act_ref[rows, 0:inner].astype(F32) * spread_heads(col_scale, spread, 2)).astype(BF16)
        ady = (grad_ref[rows, :].astype(F32) * spread_heads(row_scale, spread, 2)).astype(BF16)
        bx_ref[rows, :] = bx
        ady_ref[rows, :] = ady
        keys = (act_ref[rows, inner : inner + STATE].astype(F32) * tail).astype(BF16)
        queries = (act_ref[rows, inner + STATE : inner + 2 * STATE].astype(F32) * alive).astype(BF16)
        fresh.append(mm_tn(keys, bx) * half_wide)
        back.append(mm_tn(queries, ady) * half_wide)
        passing.append(through_wide)
    copies[10].start()
    copies[11].start()
    up = fresh[0]
    for block in range(1, blocks):
        up = passing[block] * up + fresh[block]
    down = back[blocks - 1]
    for block in range(blocks - 2, -1, -1):
        down = passing[block] * down + back[block]
    for place, source in enumerate(NEAR):
        rows = slice(source * ROWS, (source + 1) * ROWS)
        pack_ref[place, :, 0:inner] = jnp.concatenate([up[rows], down[rows]], axis=0).astype(BF16)
    row = lax.broadcasted_iota(jnp.int32, (heads, EXTRA), 0)
    lane = lax.broadcasted_iota(jnp.int32, (heads, EXTRA), 1)
    wide = jnp.sum(jnp.where(row == lane, passing_heads, 0.0), axis=0, keepdims=True)
    pack_ref[:, :, inner : inner + EXTRA] = jnp.broadcast_to(
        stacked(wide, 2 * ROWS)[None], (SPLIT, 2 * ROWS, EXTRA)
    )
    copies[12].start()
    for copy in copies[9:]:
        copy.wait()


def stacked(value, rows):
    hi, mid, lo = [piece.astype(F32) for piece in pieces_of(value, 3)]
    line = lax.broadcasted_iota(jnp.int32, (rows, EXTRA), 0)
    return jnp.where(line == 0, hi, jnp.where(line == 1, mid, jnp.where(line == 2, lo, 0.0))).astype(BF16)


def passed(pack_ref, source, inner, spread):
    lines = pack_ref[source, 0:16, inner : inner + EXTRA]
    return (
        jnp.sum(lines.astype(F32), axis=0, keepdims=True),
        jnp.sum(mm(lines, spread), axis=0, keepdims=True),
    )


def near_place(place):
    return NEAR.index(place)


def far_place(group):
    return (group + SPLIT // 2) % SPLIT


def totals_kernel(near_ref, out_ref):
    inner = near_ref.shape[2] - EXTRA
    group = lax.axis_index("ch")
    spread = spread_matrix(EXTRA, inner)
    decay = [passed(near_ref, near_place(source), inner, spread) for source in range(SPLIT)]
    up = jnp.zeros((ROWS, inner), F32)
    down = jnp.zeros((ROWS, inner), F32)
    through = jnp.ones((1, EXTRA), F32)
    for source in range(SPLIT):
        up = decay[source][1] * up + near_ref[near_place(source), 0:ROWS, 0:inner].astype(F32)
        through = through * decay[source][0]
    for source in range(SPLIT - 1, -1, -1):
        down = decay[source][1] * down + near_ref[near_place(source), ROWS : 2 * ROWS, 0:inner].astype(F32)
    lines = stacked(through, ROWS)
    for target in range(SPLIT):
        later = jnp.where(target > group, 1.0, 0.0)
        out_ref[far_place(target), :, 0:inner] = (later * up + (1.0 - later) * down).astype(BF16)
        out_ref[far_place(target), :, inner : inner + EXTRA] = lines


def states_kernel(near_ref, far_ref, out_ref):
    inner = near_ref.shape[2] - EXTRA
    group = lax.axis_index("ch")
    spread = spread_matrix(EXTRA, inner)
    near = [passed(near_ref, near_place(source), inner, spread)[1] for source in range(SPLIT)]
    far = [passed(far_ref, far_place(source), inner, spread)[1] for source in range(SPLIT)]
    up = jnp.zeros((ROWS, inner), F32)
    down = jnp.zeros((ROWS, inner), F32)
    for source in range(SPLIT):
        use = jnp.where(source < group, 1.0, 0.0)
        up = (use * far[source] + (1.0 - use)) * up + use * far_ref[far_place(source), :, 0:inner].astype(F32)
    for source in range(SPLIT - 1, -1, -1):
        use = jnp.where(source > group, 1.0, 0.0)
        down = (use * far[source] + (1.0 - use)) * down + use * far_ref[far_place(source), :, 0:inner].astype(F32)
    for source in range(SPLIT):
        out_ref[near_place(source), 0:ROWS, :] = up.astype(BF16)
        up = near[source] * up + near_ref[near_place(source), 0:ROWS, 0:inner].astype(F32)
    for source in range(SPLIT - 1, -1, -1):
        out_ref[near_place(source), ROWS : 2 * ROWS, :] = down.astype(BF16)
        down = near[source] * down + near_ref[near_place(source), ROWS : 2 * ROWS, 0:inner].astype(F32)


def local_kernel(
    length, input_ref, rim_ref, grad_ref, raw_ref, flags_ref, power_ref, step_bias_ref, skip_ref, weight_ref, bias_ref,
    act_ref, bx_ref, ady_ref,
    dpre_ref, reach_ref, sums_ref, heads_ref, marked_ref, inside_ref, lines_ref, meets_ref, sides_ref, base_ref,
    padded, slope_ref, product,
):
    tokens, channels = act_ref.shape
    inner = bx_ref.shape[1]
    heads = inner // HEAD_WIDTH
    blocks = tokens // BLOCK
    fill_padded(padded, rim_ref[...], input_ref[...])
    weight = weight_ref[...].astype(F32)
    for low in range(0, channels, 128):
        cols = slice(low, low + 128)
        for start in range(0, tokens, 64):
            total, gate = silu_rows(padded, weight, bias_ref, start, cols)
            slope_ref[start : start + 64, cols] = gate * (1.0 + total * (1.0 - gate))
    step, rate = head_steps(raw_ref[...], step_bias_ref[...], power_ref[...], length)
    heads_ref[0:heads, :] = step
    heads_ref[heads : 2 * heads, :] = 1.0 / (1.0 + jnp.exp(-(raw_ref[...] + column(step_bias_ref[...]))))
    heads_ref[2 * heads : 3 * heads, :] = jnp.broadcast_to(rate, (heads, tokens))
    spread = spread_matrix(heads, inner)
    gather = gather_matrix(inner, heads)
    flags = flags_ref[...].astype(F32)
    skip_wide = spread_heads(jnp.broadcast_to(column(skip_ref[...]), (heads, 8)), spread, 3)[0:1]
    key_cols, query_cols = slice(inner, inner + STATE), slice(inner + STATE, channels)
    for block in range(blocks):
        rows = slice(block * BLOCK, (block + 1) * BLOCK)
        mask, alive, tail, alive_last = block_marks(flags[block : block + 1])
        _, col_scale, half, whole = block_scales(step[:, rows], rate)
        half_wide, through_wide = wide_lines(half, whole * alive_last, spread)
        lines_ref[2 * block : 2 * block + 1, :] = half_wide
        lines_ref[2 * block + 1 : 2 * block + 2, :] = through_wide
        bx = bx_ref[rows, :]
        ady = ady_ref[rows, :]
        key = act_ref[rows, key_cols]
        query = act_ref[rows, query_cols]
        keys = (key.astype(F32) * tail).astype(BF16)
        queries = (query.astype(F32) * alive).astype(BF16)
        marked_ref[rows, 0:STATE] = keys
        marked_ref[rows, STATE : 2 * STATE] = queries
        if block < blocks - 1:
            inside_ref[block] = mm_tn(keys, bx) * half_wide
        if block > 0:
            inside_ref[blocks - 2 + block] = mm_tn(queries, ady) * half_wide
        scores = mask * mm_nt(query, key)
        scores_t = scores.T.astype(BF16)
        dbx = mm(scores_t, ady)
        col_sum = exact_right(bx.astype(F32) * dbx, gather, 2)
        row_sum = exact_right(ady.astype(F32) * mm(scores.astype(BF16), bx), gather, 2)
        sums_ref[0:heads, rows] = (row_sum - col_sum).T
        sums_ref[heads : 2 * heads, rows] = col_sum.T
        dscores = mask * mm_nt(ady, bx)
        dscores_t = dscores.T.astype(BF16)
        dquery = mm(dscores.astype(BF16), key)
        dkey = mm(dscores_t, query)
        slope = slope_ref[rows, 0:inner]
        reach = slope * spread_heads(col_scale, spread, 2)
        reach_ref[rows, 0:inner] = reach
        reach_ref[rows, key_cols] = slope_ref[rows, key_cols] * tail
        reach_ref[rows, query_cols] = slope_ref[rows, query_cols] * alive
        dpre_ref[rows, 0:inner] = reach * dbx + slope * (skip_wide * grad_ref[rows, :].astype(F32))
        dpre_ref[rows, key_cols] = dkey * slope_ref[rows, key_cols]
        dpre_ref[rows, query_cols] = dquery * slope_ref[rows, query_cols]
    lines_ref[2 * blocks :, :] = jnp.zeros((lines_ref.shape[0] - 2 * blocks, inner), F32)
    line = lax.broadcasted_iota(jnp.int32, (8, 128), 0)
    for low in range(0, channels, 128):
        cols = slice(low, low + 128)
        found = jnp.zeros((8, 128), F32)
        for tap in range(KERNEL + 1):
            acc = jnp.zeros((8, 128), F32)
            for start in range(0, tokens, 64):
                rows = slice(start, start + 64)
                at = 8 - (KERNEL - 1) + start + tap
                here, meets = dpre_ref[rows, cols], reach_ref[rows, cols]
                if tap < KERNEL:
                    other = padded[at : at + 64, cols]
                    here, meets = here * other, meets * other
                acc = acc + jnp.sum(here.reshape(8, 8, 128), axis=0)
                if low < inner:
                    product[tap, rows, cols] = meets.astype(BF16)
                else:
                    sides_ref[tap, rows, low - inner : low - inner + 128] = meets.astype(BF16)
            found = jnp.where(line == tap, jnp.sum(acc, axis=0, keepdims=True), found)
        base_ref[:, cols] = found
    line = lax.broadcasted_iota(jnp.int32, (8, inner), 0)
    found = base_ref[:, 0:inner]
    for tap in range(KERNEL + 1):
        through = jnp.ones((1, inner), F32)
        own = jnp.zeros((STATE, inner), F32)
        total = jnp.zeros((STATE, inner), F32)
        for block in range(blocks - 1, -1, -1):
            rows = slice(block * BLOCK, (block + 1) * BLOCK)
            meets = mm_tn(marked_ref[rows, 0:STATE], product[tap, rows, :]) * lines_ref[2 * block : 2 * block + 1, :]
            total = total + through * meets
            if block < blocks - 1:
                found = found + jnp.where(line == tap, jnp.sum(own * meets, axis=0, keepdims=True), 0.0)
            if block > 0:
                decay = lines_ref[2 * block + 1 : 2 * block + 2, :]
                through = decay * through
                own = decay * own + inside_ref[blocks - 2 + block]
        meets_ref[tap] = total.astype(BF16)
    base_ref[:, 0:inner] = found


def block_states(carry_ref, inside_ref, lines_ref, blocks):
    entering, leaving = (
        jnp.concatenate([carry_ref[near_place(i), low : low + ROWS, :].astype(F32) for i in range(SPLIT)], axis=0)
        for low in (0, ROWS)
    )
    states, grads = [entering], [leaving]
    for block in range(blocks - 1):
        through = lines_ref[2 * block + 1 : 2 * block + 2, :]
        states.append(through * states[-1] + inside_ref[block])
    for block in range(blocks - 1, 0, -1):
        through = lines_ref[2 * block + 1 : 2 * block + 2, :]
        grads.append(through * grads[-1] + inside_ref[blocks - 2 + block])
    return states, grads[::-1]


def taps_kernel(
    carry_hbm, lines_hbm, inside_hbm, bx_hbm, ady_hbm, marked_hbm, part_hbm, reach_hbm, weight_hbm, meets_hbm, sides_hbm,
    base_hbm,
    head_ref, terms_ref,
    carry_ref, lines_ref, inside_ref, bx_ref, ady_ref, marked_ref, part_ref, reach_ref, weight_ref, meets_ref,
    sides_ref, base_ref, sums_ref, sems,
):
    top = part_ref.shape[0]
    pairs = (
        (carry_hbm, carry_ref),
        (lines_hbm, lines_ref),
        (inside_hbm, inside_ref),
        (bx_hbm, bx_ref),
        (ady_hbm, ady_ref),
        (marked_hbm.at[0:top], marked_ref),
        (part_hbm.at[0:top], part_ref),
        (reach_hbm.at[0:top], reach_ref),
        (weight_hbm, weight_ref),
        (sides_hbm, sides_ref),
        (base_hbm, base_ref),
        (meets_hbm, meets_ref),
    )
    copies = [pltpu.make_async_copy(source, target, sems.at[i]) for i, (source, target) in enumerate(pairs)]
    for copy in copies:
        copy.start()
    channels = part_ref.shape[1]
    tokens, inner = bx_ref.shape
    blocks = tokens // BLOCK
    line = lax.broadcasted_iota(jnp.int32, (8, 128), 0)
    for copy in copies[:9]:
        copy.wait()
    states, grads = block_states(carry_ref, inside_ref, lines_ref, blocks)
    keys, queries = [], []
    for block in range(blocks):
        rows = slice(block * BLOCK, (block + 1) * BLOCK)
        half = lines_ref[2 * block : 2 * block + 1, :]
        grad = (half * grads[block]).astype(BF16)
        keys.append(mm_nt(bx_ref[rows, :], grad))
        queries.append(mm_nt(ady_ref[rows, :], (half * states[block]).astype(BF16)))
        if block == 0:
            first = part_ref[:, 0:inner] + reach_ref[:, 0:inner] * mm(marked_ref[:, 0:STATE], grad)
    key_cols, query_cols = slice(inner, inner + STATE), slice(inner + STATE, channels)
    first = [
        first[0:8],
        (part_ref[:, key_cols] + reach_ref[:, key_cols] * keys[0][0:top])[0:8],
        (part_ref[:, query_cols] + reach_ref[:, query_cols] * queries[0][0:top])[0:8],
    ]
    weight = weight_ref[...].astype(F32)
    for part, cols in zip(first, (slice(0, inner), key_cols, query_cols)):
        wide = lax.broadcasted_iota(jnp.int32, part.shape, 0)
        lines = jnp.zeros(part.shape, F32)
        for at in range(KERNEL - 1):
            row = sum(weight[tap : tap + 1, cols] * part[at - tap : at - tap + 1] for tap in range(at + 1))
            lines = jnp.where(wide == at, row, lines)
        head_ref[:, cols] = lines
    for copy in copies[9:11]:
        copy.wait()
    for side, parts in enumerate((keys, queries)):
        cols = slice(side * STATE, (side + 1) * STATE)
        out = slice(inner + side * STATE, inner + (side + 1) * STATE)
        found = base_ref[:, out]
        for tap in range(KERNEL + 1):
            acc = jnp.zeros((8, STATE), F32)
            for block in range(blocks):
                rows = slice(block * BLOCK, (block + 1) * BLOCK)
                met = parts[block] * sides_ref[tap, rows, cols].astype(F32)
                acc = acc + jnp.sum(met.reshape(BLOCK // 8, 8, STATE), axis=0)
            found = found + jnp.where(line == tap, jnp.sum(acc, axis=0, keepdims=True), 0.0)
        sums_ref[:, out] = found
    copies[11].wait()
    for low in range(0, inner, 128):
        cols = slice(low, low + 128)
        grad = jnp.concatenate(
            [carry_ref[near_place(i), ROWS : 2 * ROWS, cols].astype(F32) for i in range(SPLIT)], axis=0
        )
        found = base_ref[:, cols]
        for tap in range(KERNEL + 1):
            met = grad * meets_ref[tap, :, cols].astype(F32)
            acc = jnp.sum(met.reshape(STATE // 8, 8, 128), axis=0)
            found = found + jnp.where(line == tap, jnp.sum(acc, axis=0, keepdims=True), 0.0)
        sums_ref[:, cols] = found

    targets = terms_ref.shape[0]
    width = channels // targets
    lane = lax.broadcasted_iota(jnp.int32, (8, 128), 1)
    own = (lane >= line * width) & (lane < (line + 1) * width) & (line <= KERNEL)
    for tile in range(channels // 128, sums_ref.shape[1] // 128):
        sums_ref[:, tile * 128 : tile * 128 + 128] = jnp.zeros((8, 128), F32)
    aside = pltpu.roll(sums_ref[...], 0, 1, stride=width // 2, stride_axis=0)
    sums_ref[...] = pltpu.roll(aside, 0, 1, stride=width - width // 2, stride_axis=0)
    for target in range(targets):
        tile, at = divmod(target * width, 128)
        part = sums_ref[:, tile * 128 : tile * 128 + 128]
        if at:
            part = jnp.where(lane >= at, part, sums_ref[:, tile * 128 + 128 : tile * 128 + 256])
            part = pltpu.roll(part, 128 - at, 1)
        terms_ref[target : target + 1, :] = jnp.sum(jnp.where(own, part, 0.0), axis=0, keepdims=True)


def rest_kernel(
    carry_ref, marked_ref, bx_ref, ady_ref, part_ref, reach_ref, inside_ref, lines_ref, sums_ref, heads_ref, weight_ref,
    back_ref,
    out_ref, raw_out_ref, dpre, after,
):
    tokens, channels = part_ref.shape
    inner = bx_ref.shape[1]
    heads = inner // HEAD_WIDTH
    blocks = tokens // BLOCK
    key_cols, query_cols = slice(inner, inner + STATE), slice(inner + STATE, channels)
    gather = gather_matrix(inner, heads)
    lower = triangles()[0].astype(BF16)
    at_last = jnp.where(lax.broadcasted_iota(jnp.int32, (heads, BLOCK), 1) == BLOCK - 1, 1.0, 0.0)
    states, grads = block_states(carry_ref, inside_ref, lines_ref, blocks)
    for block in range(blocks):
        rows = slice(block * BLOCK, (block + 1) * BLOCK)
        half = lines_ref[2 * block : 2 * block + 1, :]
        through = lines_ref[2 * block + 1 : 2 * block + 2, :]
        state = (half * states[block]).astype(BF16)
        grad = (half * grads[block]).astype(BF16)
        keys = marked_ref[rows, 0:STATE]
        queries = marked_ref[rows, STATE : 2 * STATE]
        bx = bx_ref[rows, :]
        ady = ady_ref[rows, :]
        dbx = mm(keys, grad)
        dpre[rows, 0:inner] = part_ref[rows, 0:inner] + reach_ref[rows, 0:inner] * dbx
        dpre[rows, key_cols] = part_ref[rows, key_cols] + reach_ref[rows, key_cols] * mm_nt(bx, grad)
        dpre[rows, query_cols] = part_ref[rows, query_cols] + reach_ref[rows, query_cols] * mm_nt(ady, state)
        row_sum = exact_right(ady.astype(F32) * mm(queries, state), gather, 2)
        col_sum = exact_right(bx.astype(F32) * dbx, gather, 2)
        whole = jnp.sum(
            grad.astype(F32) * mm_tn(keys, bx) + through * (grads[block] * states[block]), axis=0, keepdims=True
        )
        whole = exact_right(jnp.broadcast_to(whole, (8, inner)), gather, 3)
        dcum = sums_ref[0:heads, rows] + (row_sum - col_sum).T + at_last * column(whole[0:1])
        dlog = exact_right(dcum, lower, 3)
        step, gate, rate = (heads_ref[i * heads : (i + 1) * heads, rows] for i in range(3))
        raw_out_ref[:, rows] = ((sums_ref[heads : 2 * heads, rows] + col_sum.T) / step + rate * dlog) * gate
    dpre[tokens : tokens + 8, :] = jnp.zeros((8, channels), F32)
    after[...] = jnp.zeros((8, channels), F32)
    after[8 - (KERNEL - 1) : 8, :] = back_ref[...]
    weight = weight_ref[...].astype(F32)
    for low in range(0, channels, 128):
        cols = slice(low, low + 128)
        for start in range(0, tokens, 64):
            total = dpre[start : start + 64, cols] * weight[KERNEL - 1 : KERNEL, cols]
            for tap in range(KERNEL - 1):
                ahead = start + KERNEL - 1 - tap
                total = total + dpre[ahead : ahead + 64, cols] * weight[tap : tap + 1, cols]
            if start == tokens - 64:
                total = jnp.concatenate([total[0:56], total[56:64] + after[:, cols]], axis=0)
            out_ref[start : start + 64, cols] = total.astype(BF16)


def shares_kernel(scale, terms_ref, weight_ref, bias_ref):
    total = jnp.sum(terms_ref[...], axis=0) * scale
    width = bias_ref.shape[1]
    for tap in range(KERNEL):
        weight_ref[tap, :, :] = total[:, tap * width : (tap + 1) * width]
    bias_ref[...] = total[:, KERNEL * width : (KERNEL + 1) * width]


def call(kernel, out_shape, scratch=(), flops=0, moved=0, vmem=WIDE, **specs):
    return pl.pallas_call(
        kernel,
        out_shape=out_shape,
        scratch_shapes=list(scratch),
        compiler_params=pltpu.CompilerParams(vmem_limit_bytes=vmem),
        cost_estimate=pl.CostEstimate(flops=flops, bytes_accessed=moved, transcendentals=0),
        **specs,
    )


def shifted(value, axis, by):
    devices = lax.axis_size(axis)
    pairs = [(i, i + by) for i in range(devices) if 0 <= i + by < devices]
    return lax.ppermute(value, axis, pairs)


def body(
    conv_input, step_raw, doc_starts, decay_power, conv_weight, conv_bias, step_bias, skip_gain, grad_out
):
    tokens, channels = conv_input.shape[1:]
    heads = step_raw.shape[2]
    inner = heads * HEAD_WIDTH
    ctx_size = lax.axis_size(CTX)
    dp_size = lax.axis_size("dp")
    devices = dp_size * ctx_size
    length = tokens * ctx_size
    inputs = conv_input[0]
    rim = shifted(inputs[tokens - (KERNEL - 1) :], CTX, 1)
    blocks = tokens // BLOCK
    shape = jax.ShapeDtypeStruct
    padded = pltpu.VMEM((tokens + 8, channels), F32)
    placed = pl.BlockSpec(memory_space=pltpu.HBM)
    held = pl.BlockSpec(memory_space=pltpu.VMEM)
    grads = grad_out[0]
    raw = step_raw[0].T
    flags = doc_starts.reshape(blocks, BLOCK)
    power, step_bias, skip, bias = decay_power[None], step_bias[None], skip_gain[None], conv_bias[None]

    def buffers(*arrays):
        return [pltpu.VMEM(array.shape, array.dtype) for array in arrays]

    sources = (inputs, rim, grads, raw, flags, power, step_bias, conv_weight, bias)
    results = (
        shape((tokens, channels), BF16),
        shape((tokens, inner), BF16),
        shape((tokens, inner), BF16),
        shape((SPLIT, 2 * ROWS, inner + EXTRA), BF16),
    )
    act, bx, ady, pack = call(
        lambda *refs: front_kernel(length, *refs),
        results,
        buffers(*sources, *results) + [padded, pltpu.SemaphoreType.DMA((len(sources) + len(results),))],
        in_specs=[placed] * len(sources),
        out_specs=(placed,) * len(results),
    )(*sources)

    part, reach, sums, per_head, marked, inside, lines, meets, sides, base = call(
        lambda *refs: local_kernel(length, *refs),
        (
            shape((tokens, channels), F32),
            shape((tokens, channels), F32),
            shape((2 * heads, tokens), F32),
            shape((3 * heads, tokens), F32),
            shape((tokens, 2 * STATE), BF16),
            shape((2 * (blocks - 1), STATE, inner), F32),
            shape((8, inner), F32),
            shape((KERNEL + 1, STATE, inner), BF16),
            shape((KERNEL + 1, tokens, 2 * STATE), BF16),
            shape((8, channels), F32),
        ),
        [padded, pltpu.VMEM((tokens, channels), F32), pltpu.VMEM((KERNEL + 1, tokens, inner), BF16)],
        flops=10**9,
        moved=10**7,
    )(inputs, rim, grads, raw, flags, power, step_bias, skip, conv_weight, bias, act, bx, ady)

    near = lax.all_to_all(pack, "cl", 0, 0, tiled=True, axis_index_groups=[list(NEAR)])
    near, lines = lax.optimization_barrier((near, lines))
    totals = call(totals_kernel, shape((SPLIT, ROWS, inner + EXTRA), BF16), vmem=NARROW)(near)
    turned = [[far_place(place) for place in range(SPLIT)]]
    far = lax.all_to_all(totals, "ch", 0, 0, tiled=True, axis_index_groups=turned)
    states = call(
        states_kernel,
        shape((SPLIT, 2 * ROWS, inner), BF16),
        vmem=NARROW,
    )(near, far)
    carry = lax.all_to_all(states, "cl", 0, 0, tiled=True, axis_index_groups=[list(NEAR)])

    sources = (carry, lines, inside, bx, ady, marked, part, reach, conv_weight, meets, sides, base)
    tops = [shape((16,) + a.shape[1:], a.dtype) if a is marked or a is part or a is reach else a for a in sources]
    head, terms = call(
        taps_kernel,
        (shape((8, channels), F32), shape((devices, 128), F32)),
        buffers(*tops) + [pltpu.VMEM((8, channels + 2 * 128), F32), pltpu.SemaphoreType.DMA((len(sources),))],
        in_specs=[placed] * len(sources),
    )(*sources)

    terms = lax.all_to_all(terms.reshape(devices, 1, 128), ("dp",) + CTX, 0, 0, tiled=True)
    back = shifted(head[: KERNEL - 1], CTX, -1)
    out, grad_raw = call(
        rest_kernel,
        (shape((tokens, channels), BF16), shape((heads, tokens), F32)),
        [padded, pltpu.VMEM((8, channels), F32)],
        flops=10**9,
        moved=10**7,
    )(carry, marked, bx, ady, part, reach, inside, lines, sums, per_head, conv_weight, back)
    width = channels // devices
    grad_weight, grad_bias = call(
        lambda *refs: shares_kernel(1.0 / (dp_size * length), *refs),
        (shape((KERNEL, 1, width), F32), shape((1, width), F32)),
        vmem=NARROW,
    )(terms)
    return (out[None], grad_raw.T[None], grad_weight, grad_bias)


def solution(mesh):
    sizes = mesh.shape
    shape = (sizes["dp"], sizes["ctx"] // SPLIT, SPLIT, sizes["tp"])
    mesh = jax.sharding.Mesh(mesh.devices.reshape(shape), ("dp",) + CTX + ("tp",))
    return jax.shard_map(
        body,
        mesh=mesh,
        in_specs=(
            P("dp", CTX, "tp"),
            P("dp", CTX, "tp"),
            P("dp", CTX),
            P("tp"),
            P(None, "tp"),
            P("tp"),
            P("tp"),
            P("tp"),
            P("dp", CTX, "tp"),
        ),
        out_specs=(
            P("dp", CTX, "tp"),
            P("dp", CTX, "tp"),
            P(None, "tp", ("dp",) + CTX),
            P("tp", ("dp",) + CTX),
        ),
        check_vma=False,
    )
```

```python
import math

import jax
import jax.numpy as jnp
from jax import lax
from jax.experimental import pallas as pl
from jax.experimental.pallas import tpu as pltpu
from jax.sharding import PartitionSpec as P

BLOCK = 128
HEAD_WIDTH = 64
STATE = 128
KERNEL = 4
SPLIT = 4
ROWS = STATE // SPLIT
EXTRA = 128
WIDE = 60 * 1024 * 1024
NARROW = 16 * 1024 * 1024
F32 = jnp.float32
BF16 = jnp.bfloat16
CTX = ("ch", "cl")
NEAR = (2, 1, 0, 3)


def mm(left, right):
    return jnp.dot(left, right, preferred_element_type=F32)


def mm_nt(left, right):
    return lax.dot_general(left, right, (((1,), (1,)), ((), ())), preferred_element_type=F32)


def mm_tn(left, right):
    return lax.dot_general(left, right, (((0,), (0,)), ((), ())), preferred_element_type=F32)


def pieces_of(value, count):
    out = []
    for _ in range(count):
        piece = value.astype(BF16)
        out.append(piece)
        value = value - piece.astype(F32)
    return out


def exact_left(ones, value, count):
    return sum(mm(ones, piece) for piece in pieces_of(value, count))


def exact_right(value, ones, count):
    return sum(mm(piece, ones) for piece in pieces_of(value, count))


def spread_matrix(rows, columns):
    row = lax.broadcasted_iota(jnp.int32, (rows, columns), 0)
    lane = lax.broadcasted_iota(jnp.int32, (rows, columns), 1)
    return jnp.where((lane >> 6) == row, 1.0, 0.0).astype(BF16)


def gather_matrix(rows, columns):
    row = lax.broadcasted_iota(jnp.int32, (rows, columns), 0)
    lane = lax.broadcasted_iota(jnp.int32, (rows, columns), 1)
    return jnp.where((row >> 6) == lane, 1.0, 0.0).astype(BF16)


def spread_heads(value, spread, count):
    return sum(mm_tn(piece, spread) for piece in pieces_of(value, count))


def column(line):
    heads = line.shape[1]
    row = lax.broadcasted_iota(jnp.int32, (heads, heads), 0)
    lane = lax.broadcasted_iota(jnp.int32, (heads, heads), 1)
    return jnp.sum(jnp.where(row == lane, line, jnp.zeros_like(line)), axis=1, keepdims=True)


def softplus(value):
    small = jnp.exp(-jnp.abs(value))
    series = small * (1.0 - small * (0.5 - small * (1.0 / 3.0 - small * 0.25)))
    return jnp.maximum(value, 0.0) + jnp.where(small < 0.01, series, jnp.log(1.0 + small))


def triangles():
    row = lax.broadcasted_iota(jnp.int32, (BLOCK, BLOCK), 0)
    lane = lax.broadcasted_iota(jnp.int32, (BLOCK, BLOCK), 1)
    return jnp.where(row >= lane, 1.0, 0.0), jnp.where(row <= lane, 1.0, 0.0)


def block_marks(flags):
    lower, upper = triangles()
    seg_col = jnp.sum(lower * flags, axis=1, keepdims=True)
    seg_row = mm(jnp.broadcast_to(flags, (8, BLOCK)).astype(BF16), upper.astype(BF16))[0:1]
    last = jnp.sum(flags, axis=1, keepdims=True)
    mask = jnp.where(seg_col == seg_row, lower, 0.0)
    alive = jnp.where(seg_col == 0.0, 1.0, 0.0)
    tail = jnp.where(seg_col == last, 1.0, 0.0)
    alive_last = jnp.where(last == 0.0, 1.0, 0.0)
    return mask, alive, tail, alive_last


def head_steps(raw, bias, power, length):
    rate = -0.5 * jnp.exp((power.astype(F32) / 3.0 - 1.0) * math.log(length))
    return softplus(raw + column(bias)), column(rate)


def block_scales(step, rate):
    upper = triangles()[1].astype(BF16)
    cum = exact_right(step * rate, upper, 3)
    total = cum[:, BLOCK - 1 : BLOCK]
    middle = 0.5 * total
    return jnp.exp(cum - middle), step * jnp.exp(middle - cum), jnp.exp(middle), jnp.exp(total)


def wide_lines(half, through, spread):
    lane = lax.broadcasted_iota(jnp.int32, (half.shape[0], 8), 1)
    lines = spread_heads(jnp.where(lane == 0, half, through), spread, 3)
    return lines[0:1], lines[1:2]


def silu_rows(padded, weight, bias_ref, start, cols):
    total = jnp.broadcast_to(bias_ref[:, cols], (64, 128))
    for tap in range(KERNEL):
        at = 8 - (KERNEL - 1) + start + tap
        total = total + padded[at : at + 64, cols] * weight[tap : tap + 1, cols]
    return total, 1.0 / (1.0 + jnp.exp(-total))


def fill_padded(padded, rim, inputs):
    tokens, channels = inputs.shape
    padded[0:8, :] = jnp.zeros((8, channels), F32)
    padded[8 - (KERNEL - 1) : 8, :] = rim.astype(F32)
    padded[8 : 8 + tokens, :] = inputs.astype(F32)


def front_kernel(
    length, input_hbm, rim_hbm, grad_hbm, raw_hbm, flags_hbm, power_hbm, step_bias_hbm, weight_hbm, bias_hbm,
    act_hbm, bx_hbm, ady_hbm, pack_hbm,
    input_ref, rim_ref, grad_ref, raw_ref, flags_ref, power_ref, step_bias_ref, weight_ref, bias_ref,
    act_ref, bx_ref, ady_ref, pack_ref, padded, sems,
):
    pairs = (
        (raw_hbm, raw_ref),
        (step_bias_hbm, step_bias_ref),
        (power_hbm, power_ref),
        (flags_hbm, flags_ref),
        (input_hbm, input_ref),
        (rim_hbm, rim_ref),
        (weight_hbm, weight_ref),
        (bias_hbm, bias_ref),
        (grad_hbm, grad_ref),
        (act_ref, act_hbm),
        (bx_ref, bx_hbm),
        (ady_ref, ady_hbm),
        (pack_ref, pack_hbm),
    )
    copies = [pltpu.make_async_copy(source, target, sems.at[i]) for i, (source, target) in enumerate(pairs)]
    for copy in copies[:9]:
        copy.start()
    tokens, channels = input_ref.shape
    heads = raw_ref.shape[0]
    inner = heads * HEAD_WIDTH
    blocks = tokens // BLOCK
    spread = spread_matrix(heads, inner)
    for copy in copies[:4]:
        copy.wait()
    step, rate = head_steps(raw_ref[...], step_bias_ref[...], power_ref[...], length)
    flags = flags_ref[...].astype(F32)
    marks = [block_marks(flags[block : block + 1]) for block in range(blocks)]
    scales = [block_scales(step[:, block * BLOCK : (block + 1) * BLOCK], rate) for block in range(blocks)]
    for copy in copies[4:8]:
        copy.wait()
    fill_padded(padded, rim_ref[...], input_ref[...])
    weight = weight_ref[...].astype(F32)
    for low in range(0, channels, 128):
        cols = slice(low, low + 128)
        for start in range(0, tokens, 64):
            total, gate = silu_rows(padded, weight, bias_ref, start, cols)
            act_ref[start : start + 64, cols] = (total * gate).astype(BF16)
    copies[9].start()
    copies[8].wait()
    fresh, back, passing = [], [], []
    passing_heads = jnp.ones((heads, 1), F32)
    for block in range(blocks):
        rows = slice(block * BLOCK, (block + 1) * BLOCK)
        _, alive, tail, alive_last = marks[block]
        row_scale, col_scale, half, whole = scales[block]
        through = whole * alive_last
        passing_heads = passing_heads * through
        half_wide, through_wide = wide_lines(half, through, spread)
        bx = (act_ref[rows, 0:inner].astype(F32) * spread_heads(col_scale, spread, 2)).astype(BF16)
        ady = (grad_ref[rows, :].astype(F32) * spread_heads(row_scale, spread, 2)).astype(BF16)
        bx_ref[rows, :] = bx
        ady_ref[rows, :] = ady
        keys = (act_ref[rows, inner : inner + STATE].astype(F32) * tail).astype(BF16)
        queries = (act_ref[rows, inner + STATE : inner + 2 * STATE].astype(F32) * alive).astype(BF16)
        fresh.append(mm_tn(keys, bx) * half_wide)
        back.append(mm_tn(queries, ady) * half_wide)
        passing.append(through_wide)
    copies[10].start()
    copies[11].start()
    up = fresh[0]
    for block in range(1, blocks):
        up = passing[block] * up + fresh[block]
    down = back[blocks - 1]
    for block in range(blocks - 2, -1, -1):
        down = passing[block] * down + back[block]
    for place, source in enumerate(NEAR):
        rows = slice(source * ROWS, (source + 1) * ROWS)
        pack_ref[place, :, 0:inner] = jnp.concatenate([up[rows], down[rows]], axis=0).astype(BF16)
    row = lax.broadcasted_iota(jnp.int32, (heads, EXTRA), 0)
    lane = lax.broadcasted_iota(jnp.int32, (heads, EXTRA), 1)
    wide = jnp.sum(jnp.where(row == lane, passing_heads, 0.0), axis=0, keepdims=True)
    pack_ref[:, :, inner : inner + EXTRA] = jnp.broadcast_to(
        stacked(wide, 2 * ROWS)[None], (SPLIT, 2 * ROWS, EXTRA)
    )
    copies[12].start()
    for copy in copies[9:]:
        copy.wait()


def stacked(value, rows):
    hi, mid, lo = [piece.astype(F32) for piece in pieces_of(value, 3)]
    line = lax.broadcasted_iota(jnp.int32, (rows, EXTRA), 0)
    return jnp.where(line == 0, hi, jnp.where(line == 1, mid, jnp.where(line == 2, lo, 0.0))).astype(BF16)


def passed(pack_ref, source, inner, spread):
    lines = pack_ref[source, 0:16, inner : inner + EXTRA]
    return (
        jnp.sum(lines.astype(F32), axis=0, keepdims=True),
        jnp.sum(mm(lines, spread), axis=0, keepdims=True),
    )


def near_place(place):
    return NEAR.index(place)


def far_place(group):
    return (group + SPLIT // 2) % SPLIT


def totals_kernel(near_ref, out_ref):
    inner = near_ref.shape[2] - EXTRA
    group = lax.axis_index("ch")
    spread = spread_matrix(EXTRA, inner)
    decay = [passed(near_ref, near_place(source), inner, spread) for source in range(SPLIT)]
    up = jnp.zeros((ROWS, inner), F32)
    down = jnp.zeros((ROWS, inner), F32)
    through = jnp.ones((1, EXTRA), F32)
    for source in range(SPLIT):
        up = decay[source][1] * up + near_ref[near_place(source), 0:ROWS, 0:inner].astype(F32)
        through = through * decay[source][0]
    for source in range(SPLIT - 1, -1, -1):
        down = decay[source][1] * down + near_ref[near_place(source), ROWS : 2 * ROWS, 0:inner].astype(F32)
    lines = stacked(through, ROWS)
    for target in range(SPLIT):
        later = jnp.where(target > group, 1.0, 0.0)
        out_ref[far_place(target), :, 0:inner] = (later * up + (1.0 - later) * down).astype(BF16)
        out_ref[far_place(target), :, inner : inner + EXTRA] = lines


def states_kernel(near_ref, far_ref, out_ref):
    inner = near_ref.shape[2] - EXTRA
    group = lax.axis_index("ch")
    spread = spread_matrix(EXTRA, inner)
    near = [passed(near_ref, near_place(source), inner, spread)[1] for source in range(SPLIT)]
    far = [passed(far_ref, far_place(source), inner, spread)[1] for source in range(SPLIT)]
    up = jnp.zeros((ROWS, inner), F32)
    down = jnp.zeros((ROWS, inner), F32)
    for source in range(SPLIT):
        use = jnp.where(source < group, 1.0, 0.0)
        up = (use * far[source] + (1.0 - use)) * up + use * far_ref[far_place(source), :, 0:inner].astype(F32)
    for source in range(SPLIT - 1, -1, -1):
        use = jnp.where(source > group, 1.0, 0.0)
        down = (use * far[source] + (1.0 - use)) * down + use * far_ref[far_place(source), :, 0:inner].astype(F32)
    for source in range(SPLIT):
        out_ref[near_place(source), 0:ROWS, :] = up.astype(BF16)
        up = near[source] * up + near_ref[near_place(source), 0:ROWS, 0:inner].astype(F32)
    for source in range(SPLIT - 1, -1, -1):
        out_ref[near_place(source), ROWS : 2 * ROWS, :] = down.astype(BF16)
        down = near[source] * down + near_ref[near_place(source), ROWS : 2 * ROWS, 0:inner].astype(F32)


def local_kernel(
    length, input_ref, rim_ref, grad_ref, raw_ref, flags_ref, power_ref, step_bias_ref, skip_ref, weight_ref, bias_ref,
    act_ref, bx_ref, ady_ref,
    dpre_ref, reach_ref, sums_ref, heads_ref, marked_ref, inside_ref, lines_ref, meets_ref, sides_ref, base_ref,
    padded, slope_ref, product,
):
    tokens, channels = act_ref.shape
    inner = bx_ref.shape[1]
    heads = inner // HEAD_WIDTH
    blocks = tokens // BLOCK
    fill_padded(padded, rim_ref[...], input_ref[...])
    weight = weight_ref[...].astype(F32)
    for low in range(0, channels, 128):
        cols = slice(low, low + 128)
        for start in range(0, tokens, 64):
            total, gate = silu_rows(padded, weight, bias_ref, start, cols)
            slope_ref[start : start + 64, cols] = gate * (1.0 + total * (1.0 - gate))
    step, rate = head_steps(raw_ref[...], step_bias_ref[...], power_ref[...], length)
    heads_ref[0:heads, :] = step
    heads_ref[heads : 2 * heads, :] = 1.0 / (1.0 + jnp.exp(-(raw_ref[...] + column(step_bias_ref[...]))))
    heads_ref[2 * heads : 3 * heads, :] = jnp.broadcast_to(rate, (heads, tokens))
    spread = spread_matrix(heads, inner)
    gather = gather_matrix(inner, heads)
    flags = flags_ref[...].astype(F32)
    skip_wide = spread_heads(jnp.broadcast_to(column(skip_ref[...]), (heads, 8)), spread, 3)[0:1]
    key_cols, query_cols = slice(inner, inner + STATE), slice(inner + STATE, channels)
    for block in range(blocks):
        rows = slice(block * BLOCK, (block + 1) * BLOCK)
        mask, alive, tail, alive_last = block_marks(flags[block : block + 1])
        _, col_scale, half, whole = block_scales(step[:, rows], rate)
        half_wide, through_wide = wide_lines(half, whole * alive_last, spread)
        lines_ref[2 * block : 2 * block + 1, :] = half_wide
        lines_ref[2 * block + 1 : 2 * block + 2, :] = through_wide
        bx = bx_ref[rows, :]
        ady = ady_ref[rows, :]
        key = act_ref[rows, key_cols]
        query = act_ref[rows, query_cols]
        keys = (key.astype(F32) * tail).astype(BF16)
        queries = (query.astype(F32) * alive).astype(BF16)
        marked_ref[rows, 0:STATE] = keys
        marked_ref[rows, STATE : 2 * STATE] = queries
        if block < blocks - 1:
            inside_ref[block] = mm_tn(keys, bx) * half_wide
        if block > 0:
            inside_ref[blocks - 2 + block] = mm_tn(queries, ady) * half_wide
        scores = mask * mm_nt(query, key)
        scores_t = scores.T.astype(BF16)
        dbx = mm(scores_t, ady)
        col_sum = exact_right(bx.astype(F32) * dbx, gather, 2)
        row_sum = exact_right(ady.astype(F32) * mm(scores.astype(BF16), bx), gather, 2)
        sums_ref[0:heads, rows] = (row_sum - col_sum).T
        sums_ref[heads : 2 * heads, rows] = col_sum.T
        dscores = mask * mm_nt(ady, bx)
        dscores_t = dscores.T.astype(BF16)
        dquery = mm(dscores.astype(BF16), key)
        dkey = mm(dscores_t, query)
        slope = slope_ref[rows, 0:inner]
        reach = slope * spread_heads(col_scale, spread, 2)
        reach_ref[rows, 0:inner] = reach
        reach_ref[rows, key_cols] = slope_ref[rows, key_cols] * tail
        reach_ref[rows, query_cols] = slope_ref[rows, query_cols] * alive
        dpre_ref[rows, 0:inner] = reach * dbx + slope * (skip_wide * grad_ref[rows, :].astype(F32))
        dpre_ref[rows, key_cols] = dkey * slope_ref[rows, key_cols]
        dpre_ref[rows, query_cols] = dquery * slope_ref[rows, query_cols]
    lines_ref[2 * blocks :, :] = jnp.zeros((lines_ref.shape[0] - 2 * blocks, inner), F32)
    line = lax.broadcasted_iota(jnp.int32, (8, 128), 0)
    for low in range(0, channels, 128):
        cols = slice(low, low + 128)
        found = jnp.zeros((8, 128), F32)
        for tap in range(KERNEL + 1):
            acc = jnp.zeros((8, 128), F32)
            for start in range(0, tokens, 64):
                rows = slice(start, start + 64)
                at = 8 - (KERNEL - 1) + start + tap
                here, meets = dpre_ref[rows, cols], reach_ref[rows, cols]
                if tap < KERNEL:
                    other = padded[at : at + 64, cols]
                    here, meets = here * other, meets * other
                acc = acc + jnp.sum(here.reshape(8, 8, 128), axis=0)
                if low < inner:
                    product[tap, rows, cols] = meets.astype(BF16)
                else:
                    sides_ref[tap, rows, low - inner : low - inner + 128] = meets.astype(BF16)
            found = jnp.where(line == tap, jnp.sum(acc, axis=0, keepdims=True), found)
        base_ref[:, cols] = found
    line = lax.broadcasted_iota(jnp.int32, (8, inner), 0)
    found = base_ref[:, 0:inner]
    for tap in range(KERNEL + 1):
        through = jnp.ones((1, inner), F32)
        own = jnp.zeros((STATE, inner), F32)
        total = jnp.zeros((STATE, inner), F32)
        for block in range(blocks - 1, -1, -1):
            rows = slice(block * BLOCK, (block + 1) * BLOCK)
            meets = mm_tn(marked_ref[rows, 0:STATE], product[tap, rows, :]) * lines_ref[2 * block : 2 * block + 1, :]
            total = total + through * meets
            if block < blocks - 1:
                found = found + jnp.where(line == tap, jnp.sum(own * meets, axis=0, keepdims=True), 0.0)
            if block > 0:
                decay = lines_ref[2 * block + 1 : 2 * block + 2, :]
                through = decay * through
                own = decay * own + inside_ref[blocks - 2 + block]
        meets_ref[tap] = total.astype(BF16)
    base_ref[:, 0:inner] = found


def block_states(carry_ref, inside_ref, lines_ref, blocks):
    entering, leaving = (
        jnp.concatenate([carry_ref[near_place(i), low : low + ROWS, :].astype(F32) for i in range(SPLIT)], axis=0)
        for low in (0, ROWS)
    )
    states, grads = [entering], [leaving]
    for block in range(blocks - 1):
        through = lines_ref[2 * block + 1 : 2 * block + 2, :]
        states.append(through * states[-1] + inside_ref[block])
    for block in range(blocks - 1, 0, -1):
        through = lines_ref[2 * block + 1 : 2 * block + 2, :]
        grads.append(through * grads[-1] + inside_ref[blocks - 2 + block])
    return states, grads[::-1]


def taps_kernel(
    order, carry_hbm, lines_hbm, inside_hbm, bx_hbm, ady_hbm, marked_hbm, part_hbm, reach_hbm, weight_hbm, meets_hbm, sides_hbm,
    base_hbm,
    head_ref, terms_ref,
    carry_ref, lines_ref, inside_ref, bx_ref, ady_ref, marked_ref, part_ref, reach_ref, weight_ref, meets_ref,
    sides_ref, base_ref, sums_ref, sems,
):
    top = part_ref.shape[0]
    pairs = (
        (carry_hbm, carry_ref),
        (lines_hbm, lines_ref),
        (inside_hbm, inside_ref),
        (bx_hbm, bx_ref),
        (ady_hbm, ady_ref),
        (marked_hbm.at[0:top], marked_ref),
        (part_hbm.at[0:top], part_ref),
        (reach_hbm.at[0:top], reach_ref),
        (weight_hbm, weight_ref),
        (sides_hbm, sides_ref),
        (base_hbm, base_ref),
        (meets_hbm, meets_ref),
    )
    copies = [pltpu.make_async_copy(source, target, sems.at[i]) for i, (source, target) in enumerate(pairs)]
    for copy in copies:
        copy.start()
    channels = part_ref.shape[1]
    tokens, inner = bx_ref.shape
    blocks = tokens // BLOCK
    line = lax.broadcasted_iota(jnp.int32, (8, 128), 0)
    for copy in copies[:9]:
        copy.wait()
    states, grads = block_states(carry_ref, inside_ref, lines_ref, blocks)
    keys, queries = [], []
    for block in range(blocks):
        rows = slice(block * BLOCK, (block + 1) * BLOCK)
        half = lines_ref[2 * block : 2 * block + 1, :]
        grad = (half * grads[block]).astype(BF16)
        keys.append(mm_nt(bx_ref[rows, :], grad))
        queries.append(mm_nt(ady_ref[rows, :], (half * states[block]).astype(BF16)))
        if block == 0:
            first = part_ref[:, 0:inner] + reach_ref[:, 0:inner] * mm(marked_ref[:, 0:STATE], grad)
    key_cols, query_cols = slice(inner, inner + STATE), slice(inner + STATE, channels)
    first = [
        first[0:8],
        (part_ref[:, key_cols] + reach_ref[:, key_cols] * keys[0][0:top])[0:8],
        (part_ref[:, query_cols] + reach_ref[:, query_cols] * queries[0][0:top])[0:8],
    ]
    weight = weight_ref[...].astype(F32)
    for part, cols in zip(first, (slice(0, inner), key_cols, query_cols)):
        wide = lax.broadcasted_iota(jnp.int32, part.shape, 0)
        lines = jnp.zeros(part.shape, F32)
        for at in range(KERNEL - 1):
            row = sum(weight[tap : tap + 1, cols] * part[at - tap : at - tap + 1] for tap in range(at + 1))
            lines = jnp.where(wide == at, row, lines)
        head_ref[:, cols] = lines
    for copy in copies[9:11]:
        copy.wait()
    for side, parts in enumerate((keys, queries)):
        cols = slice(side * STATE, (side + 1) * STATE)
        out = slice(inner + side * STATE, inner + (side + 1) * STATE)
        found = base_ref[:, out]
        for tap in range(KERNEL + 1):
            acc = jnp.zeros((8, STATE), F32)
            for block in range(blocks):
                rows = slice(block * BLOCK, (block + 1) * BLOCK)
                met = parts[block] * sides_ref[tap, rows, cols].astype(F32)
                acc = acc + jnp.sum(met.reshape(BLOCK // 8, 8, STATE), axis=0)
            found = found + jnp.where(line == tap, jnp.sum(acc, axis=0, keepdims=True), 0.0)
        sums_ref[:, out] = found
    copies[11].wait()
    for low in range(0, inner, 128):
        cols = slice(low, low + 128)
        grad = jnp.concatenate(
            [carry_ref[near_place(i), ROWS : 2 * ROWS, cols].astype(F32) for i in range(SPLIT)], axis=0
        )
        found = base_ref[:, cols]
        for tap in range(KERNEL + 1):
            met = grad * meets_ref[tap, :, cols].astype(F32)
            acc = jnp.sum(met.reshape(STATE // 8, 8, 128), axis=0)
            found = found + jnp.where(line == tap, jnp.sum(acc, axis=0, keepdims=True), 0.0)
        sums_ref[:, cols] = found

    targets = terms_ref.shape[0]
    width = channels // targets
    lane = lax.broadcasted_iota(jnp.int32, (8, 128), 1)
    own = (lane >= line * width) & (lane < (line + 1) * width) & (line <= KERNEL)
    for tile in range(channels // 128, sums_ref.shape[1] // 128):
        sums_ref[:, tile * 128 : tile * 128 + 128] = jnp.zeros((8, 128), F32)
    aside = pltpu.roll(sums_ref[...], 0, 1, stride=width // 2, stride_axis=0)
    sums_ref[...] = pltpu.roll(aside, 0, 1, stride=width - width // 2, stride_axis=0)
    for place, target in enumerate(order):
        tile, at = divmod(target * width, 128)
        part = sums_ref[:, tile * 128 : tile * 128 + 128]
        if at:
            part = jnp.where(lane >= at, part, sums_ref[:, tile * 128 + 128 : tile * 128 + 256])
            part = pltpu.roll(part, 128 - at, 1)
        terms_ref[place : place + 1, :] = jnp.sum(jnp.where(own, part, 0.0), axis=0, keepdims=True)


def rest_kernel(
    carry_ref, marked_ref, bx_ref, ady_ref, part_ref, reach_ref, inside_ref, lines_ref, sums_ref, heads_ref, weight_ref,
    out_ref, raw_out_ref, edge_ref, dpre,
):
    tokens, channels = part_ref.shape
    inner = bx_ref.shape[1]
    heads = inner // HEAD_WIDTH
    blocks = tokens // BLOCK
    key_cols, query_cols = slice(inner, inner + STATE), slice(inner + STATE, channels)
    gather = gather_matrix(inner, heads)
    lower = triangles()[0].astype(BF16)
    at_last = jnp.where(lax.broadcasted_iota(jnp.int32, (heads, BLOCK), 1) == BLOCK - 1, 1.0, 0.0)
    states, grads = block_states(carry_ref, inside_ref, lines_ref, blocks)
    for block in range(blocks):
        rows = slice(block * BLOCK, (block + 1) * BLOCK)
        half = lines_ref[2 * block : 2 * block + 1, :]
        through = lines_ref[2 * block + 1 : 2 * block + 2, :]
        state = (half * states[block]).astype(BF16)
        grad = (half * grads[block]).astype(BF16)
        keys = marked_ref[rows, 0:STATE]
        queries = marked_ref[rows, STATE : 2 * STATE]
        bx = bx_ref[rows, :]
        ady = ady_ref[rows, :]
        dbx = mm(keys, grad)
        dpre[rows, 0:inner] = part_ref[rows, 0:inner] + reach_ref[rows, 0:inner] * dbx
        dpre[rows, key_cols] = part_ref[rows, key_cols] + reach_ref[rows, key_cols] * mm_nt(bx, grad)
        dpre[rows, query_cols] = part_ref[rows, query_cols] + reach_ref[rows, query_cols] * mm_nt(ady, state)
        row_sum = exact_right(ady.astype(F32) * mm(queries, state), gather, 2)
        col_sum = exact_right(bx.astype(F32) * dbx, gather, 2)
        whole = jnp.sum(
            grad.astype(F32) * mm_tn(keys, bx) + through * (grads[block] * states[block]), axis=0, keepdims=True
        )
        whole = exact_right(jnp.broadcast_to(whole, (8, inner)), gather, 3)
        dcum = sums_ref[0:heads, rows] + (row_sum - col_sum).T + at_last * column(whole[0:1])
        dlog = exact_right(dcum, lower, 3)
        step, gate, rate = (heads_ref[i * heads : (i + 1) * heads, rows] for i in range(3))
        raw_out_ref[:, rows] = ((sums_ref[heads : 2 * heads, rows] + col_sum.T) / step + rate * dlog) * gate
    dpre[tokens : tokens + 8, :] = jnp.zeros((8, channels), F32)
    weight = weight_ref[...].astype(F32)
    for low in range(0, channels, 128):
        cols = slice(low, low + 128)
        for start in range(0, tokens, 64):
            total = dpre[start : start + 64, cols] * weight[KERNEL - 1 : KERNEL, cols]
            for tap in range(KERNEL - 1):
                ahead = start + KERNEL - 1 - tap
                total = total + dpre[ahead : ahead + 64, cols] * weight[tap : tap + 1, cols]
            if start == tokens - 64:
                edge_ref[:, cols] = total[48:64]
            out_ref[start : start + 64, cols] = total.astype(BF16)


def shares_kernel(scale, terms_ref, edge_ref, back_ref, held_ref, weight_ref, bias_ref, out_hbm, last, sem):
    rows = last.shape[0]
    line = lax.broadcasted_iota(jnp.int32, last.shape, 0)
    total = edge_ref[...]
    for at in range(KERNEL - 1):
        total = total + jnp.where(line == rows - (KERNEL - 1) + at, back_ref[at : at + 1, :], 0.0)
    last[...] = total.astype(BF16)
    copy = pltpu.make_async_copy(last, out_hbm.at[out_hbm.shape[0] - rows :], sem)
    copy.start()
    total = jnp.sum(terms_ref[...], axis=0) * scale
    width = bias_ref.shape[1]
    for tap in range(KERNEL):
        weight_ref[tap, :, :] = total[:, tap * width : (tap + 1) * width]
    bias_ref[...] = total[:, KERNEL * width : (KERNEL + 1) * width]
    copy.wait()


def call(kernel, out_shape, scratch=(), flops=0, moved=0, vmem=WIDE, **specs):
    return pl.pallas_call(
        kernel,
        out_shape=out_shape,
        scratch_shapes=list(scratch),
        compiler_params=pltpu.CompilerParams(vmem_limit_bytes=vmem),
        cost_estimate=pl.CostEstimate(flops=flops, bytes_accessed=moved, transcendentals=0),
        **specs,
    )


def shifted(value, axis, by):
    devices = lax.axis_size(axis)
    pairs = [(i, i + by) for i in range(devices) if 0 <= i + by < devices]
    return lax.ppermute(value, axis, pairs)


def body(
    conv_input, step_raw, doc_starts, decay_power, conv_weight, conv_bias, step_bias, skip_gain, grad_out
):
    tokens, channels = conv_input.shape[1:]
    heads = step_raw.shape[2]
    inner = heads * HEAD_WIDTH
    ctx_size = lax.axis_size(CTX)
    dp_size = lax.axis_size("dp")
    devices = dp_size * ctx_size
    length = tokens * ctx_size
    inputs = conv_input[0]
    rim = shifted(inputs[tokens - (KERNEL - 1) :], CTX, 1)
    blocks = tokens // BLOCK
    shape = jax.ShapeDtypeStruct
    padded = pltpu.VMEM((tokens + 8, channels), F32)
    placed = pl.BlockSpec(memory_space=pltpu.HBM)
    held = pl.BlockSpec(memory_space=pltpu.VMEM)
    grads = grad_out[0]
    raw = step_raw[0].T
    flags = doc_starts.reshape(blocks, BLOCK)
    power, step_bias, skip, bias = decay_power[None], step_bias[None], skip_gain[None], conv_bias[None]

    def buffers(*arrays):
        return [pltpu.VMEM(array.shape, array.dtype) for array in arrays]

    sources = (inputs, rim, grads, raw, flags, power, step_bias, conv_weight, bias)
    results = (
        shape((tokens, channels), BF16),
        shape((tokens, inner), BF16),
        shape((tokens, inner), BF16),
        shape((SPLIT, 2 * ROWS, inner + EXTRA), BF16),
    )
    act, bx, ady, pack = call(
        lambda *refs: front_kernel(length, *refs),
        results,
        buffers(*sources, *results) + [padded, pltpu.SemaphoreType.DMA((len(sources) + len(results),))],
        in_specs=[placed] * len(sources),
        out_specs=(placed,) * len(results),
    )(*sources)

    part, reach, sums, per_head, marked, inside, lines, meets, sides, base = call(
        lambda *refs: local_kernel(length, *refs),
        (
            shape((tokens, channels), F32),
            shape((tokens, channels), F32),
            shape((2 * heads, tokens), F32),
            shape((3 * heads, tokens), F32),
            shape((tokens, 2 * STATE), BF16),
            shape((2 * (blocks - 1), STATE, inner), F32),
            shape((8, inner), F32),
            shape((KERNEL + 1, STATE, inner), BF16),
            shape((KERNEL + 1, tokens, 2 * STATE), BF16),
            shape((8, channels), F32),
        ),
        [padded, pltpu.VMEM((tokens, channels), F32), pltpu.VMEM((KERNEL + 1, tokens, inner), BF16)],
        flops=10**9,
        moved=10**7,
    )(inputs, rim, grads, raw, flags, power, step_bias, skip, conv_weight, bias, act, bx, ady)

    near = lax.all_to_all(pack, "cl", 0, 0, tiled=True, axis_index_groups=[list(NEAR)])
    near, lines = lax.optimization_barrier((near, lines))
    totals = call(totals_kernel, shape((SPLIT, ROWS, inner + EXTRA), BF16), vmem=NARROW)(near)
    turned = [[far_place(place) for place in range(SPLIT)]]
    far = lax.all_to_all(totals, "ch", 0, 0, tiled=True, axis_index_groups=turned)
    states = call(
        states_kernel,
        shape((SPLIT, 2 * ROWS, inner), BF16),
        vmem=NARROW,
    )(near, far)
    carry = lax.all_to_all(states, "cl", 0, 0, tiled=True, axis_index_groups=[list(NEAR)])

    sources = (carry, lines, inside, bx, ady, marked, part, reach, conv_weight, meets, sides, base)
    tops = [shape((16,) + a.shape[1:], a.dtype) if a is marked or a is part or a is reach else a for a in sources]
    order = [
        dp * ctx_size + (place + ctx_size // 4) % ctx_size for dp in range(dp_size) for place in range(ctx_size)
    ]
    head, terms = call(
        lambda *refs: taps_kernel(order, *refs),
        (shape((8, channels), F32), shape((devices, 128), F32)),
        buffers(*tops) + [pltpu.VMEM((8, channels + 2 * 128), F32), pltpu.SemaphoreType.DMA((len(sources),))],
        in_specs=[placed] * len(sources),
    )(*sources)

    terms = lax.all_to_all(terms.reshape(devices, 1, 128), ("dp",) + CTX, 0, 0, tiled=True, axis_index_groups=[order])
    back = shifted(head[: KERNEL - 1], CTX, -1)
    out, grad_raw, edge = call(
        rest_kernel,
        (shape((tokens, channels), BF16), shape((heads, tokens), F32), shape((16, channels), F32)),
        [padded],
        flops=10**9,
        moved=10**7,
    )(carry, marked, bx, ady, part, reach, inside, lines, sums, per_head, conv_weight)
    width = channels // devices
    grad_weight, grad_bias, out = call(
        lambda *refs: shares_kernel(1.0 / (dp_size * length), *refs),
        (shape((KERNEL, 1, width), F32), shape((1, width), F32), shape((tokens, channels), BF16)),
        [pltpu.VMEM((16, channels), BF16), pltpu.SemaphoreType.DMA],
        vmem=NARROW,
        in_specs=[held, held, held, placed],
        out_specs=(held, held, placed),
        input_output_aliases={3: 2},
    )(terms, edge, back, out)
    return (out[None], grad_raw.T[None], grad_weight, grad_bias)


def solution(mesh):
    sizes = mesh.shape
    shape = (sizes["dp"], sizes["ctx"] // SPLIT, SPLIT, sizes["tp"])
    mesh = jax.sharding.Mesh(mesh.devices.reshape(shape), ("dp",) + CTX + ("tp",))
    return jax.shard_map(
        body,
        mesh=mesh,
        in_specs=(
            P("dp", CTX, "tp"),
            P("dp", CTX, "tp"),
            P("dp", CTX),
            P("tp"),
            P(None, "tp"),
            P("tp"),
            P("tp"),
            P("tp"),
            P("dp", CTX, "tp"),
        ),
        out_specs=(
            P("dp", CTX, "tp"),
            P("dp", CTX, "tp"),
            P(None, "tp", ("dp",) + CTX),
            P("tp", ("dp",) + CTX),
        ),
        check_vma=False,
    )
```
